128 devices in a mesh: dp: 4 (over y_hi, core), expert: 32 (over x, z, y_lo).
Axes of the slice: x: 4, y: 4 (y_hi: 2, y_lo: 2; y = y_hi * 2 + y_lo), z: 4, core: 2. Of those that a mesh axis runs over, the one named last changes fastest.
Arguments:
- tokens: bfloat16 [16384, 2048], P(('dp', 'expert')), may hold values from -6 to 6
- grad_out: bfloat16 [16384, 2048], P(('dp', 'expert')), may hold values from -3 to 3
- gates: float32 [16384, 2], P(('dp', 'expert')), may hold values from 0.2 to 1
- expert_ids: int32 [16384, 2], P(('dp', 'expert')), may hold values from 0 to 31, all different within a row; in each aligned block of 128 rows (0 to 127, 128 to 255, ...) at most 16 rows name the same one
- w_gate: bfloat16 [32, 2048, 4096], P('expert', None, 'dp'), may hold values from -0.125 to 0.125
- w_up: bfloat16 [32, 2048, 4096], P('expert', None, 'dp'), may hold values from -0.125 to 0.125
- w_down: bfloat16 [32, 4096, 2048], P('expert', 'dp'), may hold values from -0.09375 to 0.09375
Outputs:
- grad_tokens: bfloat16 [16384, 2048], P(('dp', 'expert'))
- grad_gate: bfloat16 [32, 2048, 4096], P('expert', None, 'dp')
- grad_up: bfloat16 [32, 2048, 4096], P('expert', None, 'dp')
- grad_down: bfloat16 [32, 4096, 2048], P('expert', 'dp')
The draws below stay inside these ranges and needn't reach their ends.
Inputs may be any that keep to these rules, and one draw needn't show every extreme that they name: `expert_ids`: each row names two different experts; among the rows of one device no expert is named by more than 16 rows.
All inputs are finite; a program needn't handle non-finite values.
Results may differ from the reference program's by a relative error of at most 0.015.
Values may be sent and summed in bfloat16 or wider, within the bound.
No kernel may reach another device: no remote copies, remote signals or barrier semaphores. Data moves between devices by JAX's collectives and lax.ppermute only.
A program may use at most 192 MiB of HBM per device.

```python
import math
import jax
import jax.numpy as jnp
import numpy as np
from jax import lax

D = 2048
HID = 4096
TOK_DEV = 128
BLOCK = 512
EXPERTS = 32
MOST = 16
TOKENS = 16384
N_DP = 4


def block_scale(stream_key, dims, shards, least, top_value):
    loudness, own = 1.0, jax.random.fold_in(stream_key, 6)
    for dim, shards_of in shards:
        steps = jnp.exp(jax.random.uniform(jax.random.fold_in(own, dim), (shards_of,), jnp.float32, least / len(shards), top_value / len(shards)))
        loudness = loudness * jnp.repeat(steps, dims[dim] // shards_of).reshape([-1 if axis == dim else 1 for axis in range(len(dims))])
    return loudness


def deal_out(key, own, number, rows, number_of, top, most, lean):
    sequence = jax.random.permutation(key, number_of)
    crowded, usual = shares(number_of, rows * top, most, lean, True), shares(number_of, rows * top, most, lean, False)
    places = jnp.arange(number_of)

    def named(lengths, offset_by):
        used = int((lengths > 0).sum())
        fixed = max(1, used // 4)
        moved = fixed + (places - fixed + offset_by * (used - fixed)) % max(1, number_of - fixed)
        return jnp.zeros((number_of,), jnp.int32).at[sequence[jnp.where(places < fixed, places, moved)]].set(jnp.asarray(lengths, jnp.int32))

    lengths = jnp.where(number % 4 == 0, named(crowded, number // 4), named(usual, number - number // 4 - 1))
    mixed = jax.random.permutation(jax.random.fold_in(own, 3), number_of)
    source_of, sink = mixed[0:number_of // 2 * 2:2], mixed[1:number_of // 2 * 2:2]
    room = jnp.minimum(lengths[source_of] - 1, most - lengths[sink]) // 2
    room = jnp.where((source_of == sequence[0]) | (sink == sequence[0]) | (lengths[sink] == 0), 0, jnp.maximum(room, 0))
    moved = jax.random.randint(jax.random.fold_in(own, 4), (number_of // 2,), 0, 1 << 20) % (room + 1)
    lengths = lengths.at[source_of].add(-moved).at[sink].add(moved)
    labels = jnp.searchsorted(jnp.cumsum(lengths), jnp.arange(rows * top), side="right").astype(jnp.int32)
    listing = labels.reshape(top, rows).T
    listing = listing[jax.random.permutation(jax.random.fold_in(own, 1), rows)]
    offset_by = jax.random.randint(jax.random.fold_in(own, 2), (rows, 1), 0, top)
    return jnp.take_along_axis(listing, (jnp.arange(top)[None, :] + offset_by) % top, axis=1)


def shares(count, total, limit, slope, full):
    weights = [(1 << 20) // math.isqrt(grade ** slope) + 1 for grade in range(1, count + 1)]
    largest = limit if full else min(limit, max(-(-total // count), total * weights[0] // sum(weights)))
    least = 1 if total - largest >= count - 1 else 0
    counts, rest = [largest] + [least] * (count - 1), total - largest - least * (count - 1)
    while rest > 0:
        free = [i for i in range(1, count) if counts[i] < largest] or [i for i in range(1, count) if counts[i] < limit]
        pool, budget = sum([weights[i] for i in free]), rest
        for i in free:
            more = min(limit - counts[i], max(1, budget * weights[i] // pool), rest)
            counts[i] = counts[i] + more
            rest = rest - more
    return np.array(counts)


def bell_draw(stream_key, extent, spread, limit, pieces=(), held_as=jnp.bfloat16):
    array = spread * jax.random.normal(stream_key, extent, jnp.float32)
    if pieces:
        array = array * block_scale(stream_key, extent, pieces, -0.22, 0.18)
    return jnp.clip(array, -limit, limit).astype(held_as)


def setup_inputs(seed: int = 0) -> dict:
    keys = jax.random.split(jax.random.key(seed), 8)
    tokens = bell_draw(keys[0], (TOKENS, D), 1.0, 6.0, ((0, 128),))
    grad_out = bell_draw(keys[1], (TOKENS, D), 0.5, 3.0, ((0, 128),))
    gates = jnp.clip(0.2 + 0.8 * jax.random.uniform(keys[2], (TOKENS, 2), jnp.float32) ** block_scale(keys[2], (TOKENS, 2), ((0, 128),), -0.2, 0.2), 0.2, 1.0)
    expert_ids_keys = jax.random.split(jax.random.fold_in(keys[3], 1), TOKENS // TOK_DEV)
    expert_ids_turns = jax.random.permutation(jax.random.fold_in(keys[3], 3), TOKENS // TOK_DEV)
    expert_ids = jax.vmap(lambda own, number: deal_out(jax.random.fold_in(keys[3], 2), own, number, TOK_DEV, EXPERTS, 2, MOST, 2))(expert_ids_keys, expert_ids_turns).reshape((TOKENS, 2))
    w_gate = bell_draw(keys[4], (EXPERTS, D, HID), D ** -0.5, 0.125, ((0, 32), (2, 4)))
    w_up = bell_draw(keys[5], (EXPERTS, D, HID), D ** -0.5, 0.125, ((0, 32), (2, 4)))
    w_down = bell_draw(keys[6], (EXPERTS, HID, D), HID ** -0.5, 0.09375, ((0, 32), (1, 4)))
    return {"tokens": tokens, "grad_out": grad_out, "gates": gates, "expert_ids": expert_ids, "w_gate": w_gate, "w_up": w_up, "w_down": w_down}


def block_terms(in_block, dy_block, gate_weight, up_weight, down_weight, quarters):
    contract_last = (((1,), (1,)), ((), ()))
    contract_rows = (((0,), (0,)), ((), ()))
    gate_pre = jnp.dot(in_block, gate_weight, preferred_element_type=jnp.float32)
    up_pre = jnp.dot(in_block, up_weight, preferred_element_type=jnp.float32)
    gate_sigmoid = jax.nn.sigmoid(gate_pre)
    silu_gate = gate_pre * gate_sigmoid
    hidden = (silu_gate * up_pre).astype(jnp.bfloat16)
    d_hidden = lax.dot_general(dy_block, down_weight, contract_last, preferred_element_type=jnp.float32)
    d_gate = (d_hidden * up_pre * gate_sigmoid * (1.0 + gate_pre * (1.0 - gate_sigmoid))).astype(jnp.bfloat16)
    d_up = (d_hidden * silu_gate).astype(jnp.bfloat16)
    quarter_width = gate_weight.shape[1] // quarters
    d_input = jnp.zeros((in_block.shape[0], gate_weight.shape[0]), jnp.float32)
    for quarter in range(quarters):
        first_unit = quarter * quarter_width
        last_unit = first_unit + quarter_width
        portion = lax.dot_general(d_gate[:, first_unit:last_unit], gate_weight[:, first_unit:last_unit], contract_last, preferred_element_type=jnp.float32)
        portion = portion + lax.dot_general(d_up[:, first_unit:last_unit], up_weight[:, first_unit:last_unit], contract_last, preferred_element_type=jnp.float32)
        d_input = d_input + lax.optimization_barrier(portion.astype(jnp.bfloat16)).astype(jnp.float32)
    grad_gate = lax.dot_general(in_block, d_gate, contract_rows, preferred_element_type=jnp.float32)
    grad_up = lax.dot_general(in_block, d_up, contract_rows, preferred_element_type=jnp.float32)
    grad_down = lax.dot_general(hidden, dy_block, contract_rows, preferred_element_type=jnp.float32)
    return d_input, (grad_gate, grad_up, grad_down)


def reference(tokens, grad_out, gates, expert_ids, w_gate, w_up, w_down):
    routes = expert_ids.reshape(-1).astype(jnp.int32)
    route_count = routes.shape[0]
    capacity = N_DP * EXPERTS * MOST
    gate_flat = gates.reshape(-1)
    model_width = tokens.shape[1]
    hid_width = w_gate.shape[2]

    def per_expert(accum, expert):
        chosen = (routes == expert).astype(jnp.int32)
        filled = jnp.sum(chosen)
        position = jnp.cumsum(chosen) - 1
        target = jnp.where(chosen > 0, position, capacity).astype(jnp.int32)
        route_of = jnp.zeros((capacity,), jnp.int32).at[target].set(jnp.arange(route_count, dtype=jnp.int32), mode="drop")
        within = jnp.arange(capacity, dtype=jnp.int32) < filled
        token_of = (route_of // 2).astype(jnp.int32)
        packed_x = jnp.where(within[:, None], tokens[token_of], jnp.zeros((), jnp.bfloat16))
        scaled = gate_flat[route_of][:, None] * grad_out[token_of].astype(jnp.float32)
        packed_dy = jnp.where(within[:, None], scaled, jnp.zeros((), jnp.float32)).astype(jnp.bfloat16)
        gate_weight = w_gate[expert]
        up_weight = w_up[expert]
        down_weight = w_down[expert]
        blocks = (filled + BLOCK - 1) // BLOCK

        def advance(block_index, carried):
            packed_dx, sum_gate, sum_up, sum_down = carried
            first_row = (block_index * BLOCK).astype(jnp.int32)
            in_block = lax.dynamic_slice_in_dim(packed_x, first_row, BLOCK, 0)
            dy_block = lax.dynamic_slice_in_dim(packed_dy, first_row, BLOCK, 0)
            d_input, grads = block_terms(in_block, dy_block, gate_weight, up_weight, down_weight, N_DP)
            packed_dx = lax.dynamic_update_slice_in_dim(packed_dx, d_input, first_row, 0)
            return packed_dx, sum_gate + grads[0], sum_up + grads[1], sum_down + grads[2]

        start_state = (jnp.zeros((capacity, model_width), jnp.float32), jnp.zeros((model_width, hid_width), jnp.float32), jnp.zeros((model_width, hid_width), jnp.float32), jnp.zeros((hid_width, model_width), jnp.float32))
        packed_dx, sum_gate, sum_up, sum_down = lax.fori_loop(0, blocks, advance, start_state)
        rounded = lax.optimization_barrier(packed_dx.astype(jnp.bfloat16)).astype(jnp.float32)
        accum = accum.at[token_of].add(jnp.where(within[:, None], rounded, jnp.zeros((), jnp.float32)))
        return accum, (sum_gate.astype(jnp.bfloat16), sum_up.astype(jnp.bfloat16), sum_down.astype(jnp.bfloat16))

    start_accum = jnp.zeros((tokens.shape[0], model_width), jnp.float32)
    accum, stacked = lax.scan(per_expert, start_accum, jnp.arange(EXPERTS, dtype=jnp.int32))
    return accum.astype(jnp.bfloat16), stacked[0], stacked[1], stacked[2]
```

```python
import jax
import jax.numpy as jnp
from jax import lax
from jax.experimental import pallas as pl
from jax.experimental.pallas import tpu as pltpu
from jax.sharding import Mesh, PartitionSpec as P

DEVICE = ("yhi", "core", "x", "z", "ylo")
EXPERT = ("x", "z", "ylo")
PEERS = ("yhi", "x", "z", "ylo")

BF16 = jnp.bfloat16
F32 = jnp.float32
RANKS = 8
ROWS = 2 * RANKS
MIB = 1024 * 1024

CONTRACT_LAST = (((1,), (1,)), ((), ()))
CONTRACT_ROWS = (((0,), (0,)), ((), ()))


def params(mib):
    return pltpu.CompilerParams(vmem_limit_bytes=mib * MIB)


def route_slots(ids_ref, experts, chunk):
    tok = ids_ref.shape[0]
    lane = lax.broadcasted_iota(jnp.int32, (tok, experts), 1)
    picks = [(ids_ref[:, k : k + 1] == lane).astype(F32) for k in range(2)]
    below = lax.broadcasted_iota(jnp.int32, (tok, tok), 1) < lax.broadcasted_iota(
        jnp.int32, (tok, tok), 0
    )
    ahead = jnp.dot(
        below.astype(BF16), (picks[0] + picks[1]).astype(BF16), preferred_element_type=F32
    )
    slots = []
    for k in range(2):
        rank = jnp.sum(ahead * picks[k], axis=1, keepdims=True).astype(jnp.int32) - chunk * RANKS
        inside = (rank >= 0) & (rank < RANKS)
        slots.append(jnp.where(inside, ids_ref[:, k : k + 1] * ROWS + rank, -1))
    return slots


def pack_kernel(chunk, experts, ids_ref, gates_ref, tok_ref, grad_ref, out_ref):
    tok = ids_ref.shape[0]
    slots = route_slots(ids_ref, experts, chunk)
    lane = lax.broadcasted_iota(jnp.int32, (tok, experts * ROWS), 1)
    x_pick = ((lane == slots[0]) | (lane == slots[1])).astype(BF16)
    packed = lax.dot_general(x_pick, tok_ref[...], CONTRACT_ROWS, preferred_element_type=F32)
    for k in range(2):
        dy = (gates_ref[:, k : k + 1] * grad_ref[...].astype(F32)).astype(BF16)
        there = jnp.where(slots[k] >= 0, slots[k] + RANKS, -1)
        dy_pick = (lane == there).astype(BF16)
        packed = packed + lax.dot_general(
            dy_pick, dy, CONTRACT_ROWS, preferred_element_type=F32
        )
    packed = packed.astype(BF16).reshape(experts, ROWS, packed.shape[1])
    out_ref[:experts] = packed
    out_ref[experts:] = packed


def pack(chunk, experts, ids, gates, tokens, grad_out):
    tok, width = tokens.shape
    cols = 512
    return pl.pallas_call(
        lambda *refs: pack_kernel(chunk, experts, *refs),
        grid=(width // cols,),
        in_specs=[
            pl.BlockSpec((tok, 2), lambda i: (0, 0)),
            pl.BlockSpec((tok, 2), lambda i: (0, 0)),
            pl.BlockSpec((tok, cols), lambda i: (0, i)),
            pl.BlockSpec((tok, cols), lambda i: (0, i)),
        ],
        out_specs=pl.BlockSpec((2 * experts, ROWS, cols), lambda i: (0, 0, i)),
        out_shape=jax.ShapeDtypeStruct((2 * experts, ROWS, width), BF16),
        compiler_params=params(48),
        cost_estimate=pl.CostEstimate(
            flops=2 * 3 * tok * experts * ROWS * width,
            bytes_accessed=12 * MIB,
            transcendentals=0,
        ),
        name="pack",
    )(ids, gates, tokens, grad_out)


def rows_kernel(
    hid_steps,
    got_ref,
    wg_ref,
    wu_ref,
    wd_ref,
    wg_rows_ref,
    wu_rows_ref,
    x_ref,
    dy_ref,
    h_ref,
    dg_ref,
    du_ref,
    dx_ref,
    dx_wide,
):
    step = pl.program_id(0)
    peers, _, width = got_ref.shape
    rows = peers * RANKS
    hid_cols = wg_ref.shape[1]
    dx_cols = wg_rows_ref.shape[0]

    @pl.when(step == 0)
    def _():
        for col in range(0, width, 512):
            both = got_ref[:, :, col : col + 512].astype(F32)
            x_ref[:, col : col + 512] = both[:, :RANKS].reshape(rows, 512).astype(BF16)
            dy_ref[:, col : col + 512] = both[:, RANKS:].reshape(rows, 512).astype(BF16)

    @pl.when(step < hid_steps)
    def _():
        x = x_ref[...]
        g = jnp.dot(x, wg_ref[...], preferred_element_type=F32)
        u = jnp.dot(x, wu_ref[...], preferred_element_type=F32)
        dh = lax.dot_general(dy_ref[...], wd_ref[...], CONTRACT_LAST, preferred_element_type=F32)
        sig = jax.nn.sigmoid(g)
        silu = g * sig
        cols = pl.ds(pl.multiple_of(step * hid_cols, hid_cols), hid_cols)
        h_ref[:, cols] = (silu * u).astype(BF16)
        dg_ref[:, cols] = (dh * u * sig * (1.0 + g * (1.0 - sig))).astype(BF16)
        du_ref[:, cols] = (dh * silu).astype(BF16)

    for part in range(width // dx_cols):

        @pl.when(step == hid_steps + part)
        def _():
            dx = lax.dot_general(
                dg_ref[...], wg_rows_ref[...], CONTRACT_LAST, preferred_element_type=F32
            )
            dx = dx + lax.dot_general(
                du_ref[...], wu_rows_ref[...], CONTRACT_LAST, preferred_element_type=F32
            )
            half, col = divmod(part * dx_cols, width // 2)
            dx_wide[:, half * RANKS : (half + 1) * RANKS, col : col + dx_cols] = dx.reshape(
                peers, RANKS, dx_cols
            )

    @pl.when(step == pl.num_programs(0) - 1)
    def _():
        dx_ref[...] = dx_wide[...].astype(BF16)


def rows_pass(got, wg, wu, wd):
    peers, _, width = got.shape
    hid = wg.shape[1]
    rows = peers * RANKS
    hid_cols, dx_cols = 256, 512
    hid_steps, dx_steps = hid // hid_cols, width // dx_cols
    first = lambda i: jnp.minimum(i, hid_steps - 1)
    second = lambda i: jnp.maximum(i - hid_steps, 0)
    whole2 = lambda r, c: pl.BlockSpec((r, c), lambda i: (0, 0))
    return pl.pallas_call(
        lambda *refs: rows_kernel(hid_steps, *refs),
        grid=(hid_steps + dx_steps,),
        in_specs=[
            pl.BlockSpec((peers, ROWS, width), lambda i: (0, 0, 0)),
            pl.BlockSpec((width, hid_cols), lambda i: (0, first(i))),
            pl.BlockSpec((width, hid_cols), lambda i: (0, first(i))),
            pl.BlockSpec((hid_cols, width), lambda i: (first(i), 0)),
            pl.BlockSpec((dx_cols, hid), lambda i: (second(i), 0)),
            pl.BlockSpec((dx_cols, hid), lambda i: (second(i), 0)),
        ],
        out_specs=[
            whole2(rows, width),
            whole2(rows, width),
            whole2(rows, hid),
            whole2(rows, hid),
            whole2(rows, hid),
            pl.BlockSpec((peers, ROWS, width // 2), lambda i: (0, 0, 0)),
        ],
        out_shape=[
            jax.ShapeDtypeStruct((rows, width), BF16),
            jax.ShapeDtypeStruct((rows, width), BF16),
            jax.ShapeDtypeStruct((rows, hid), BF16),
            jax.ShapeDtypeStruct((rows, hid), BF16),
            jax.ShapeDtypeStruct((rows, hid), BF16),
            jax.ShapeDtypeStruct((peers, ROWS, width // 2), BF16),
        ],
        scratch_shapes=[pltpu.VMEM((peers, ROWS, width // 2), F32)],
        compiler_params=params(56),
        cost_estimate=pl.CostEstimate(
            flops=2 * 5 * rows * width * hid, bytes_accessed=32 * MIB, transcendentals=rows * hid
        ),
        name="rows",
    )(got, wg, wu, wd, wg, wu)


def grads_kernel(groups, *refs):
    x, dy, h, dg, du = (refs[i * groups : (i + 1) * groups] for i in range(5))
    gate_ref, up_ref, down_ref = refs[5 * groups :]

    def total(left, right):
        acc = None
        for a, b in zip(left, right):
            term = lax.dot_general(a[...], b[...], CONTRACT_ROWS, preferred_element_type=F32)
            acc = term if acc is None else acc + term
        return acc

    gate_ref[...] = total(x, dg).astype(BF16)
    up_ref[...] = total(x, du).astype(BF16)
    down_ref[...] = total(dy, h).T.astype(BF16)


def weight_grads(groups):
    rows, width = groups[0][0].shape
    hid = groups[0][2].shape[1]
    cols = 256
    count = len(groups)
    narrow = pl.BlockSpec((rows, cols), lambda i: (0, i))
    whole = pl.BlockSpec((rows, hid), lambda i: (0, 0))
    return pl.pallas_call(
        lambda *refs: grads_kernel(count, *refs),
        grid=(width // cols,),
        in_specs=[narrow] * (2 * count) + [whole] * (3 * count),
        out_specs=[
            pl.BlockSpec((cols, hid), lambda i: (i, 0)),
            pl.BlockSpec((cols, hid), lambda i: (i, 0)),
            pl.BlockSpec((hid, cols), lambda i: (0, i)),
        ],
        out_shape=[
            jax.ShapeDtypeStruct((width, hid), BF16),
            jax.ShapeDtypeStruct((width, hid), BF16),
            jax.ShapeDtypeStruct((hid, width), BF16),
        ],
        compiler_params=params(56),
        cost_estimate=pl.CostEstimate(
            flops=2 * 3 * count * rows * width * hid, bytes_accessed=40 * MIB, transcendentals=0
        ),
        name="weight_grads",
    )(*[group[i] for i in range(5) for group in groups])


def collect_kernel(experts, ids_ref, back0_ref, back1_ref, out_ref):
    half = pl.program_id(0)
    tok = ids_ref.shape[0]
    lane = lax.broadcasted_iota(jnp.int32, (tok, experts * ROWS), 1)
    total = None
    for chunk, back in enumerate((back0_ref, back1_ref)):
        slots = route_slots(ids_ref, experts, chunk)
        pick = jnp.zeros((tok, experts * ROWS), jnp.bool_)
        for slot in slots:
            pick = pick | (lane == jnp.where(slot >= 0, slot + half * RANKS, -1))
        dx = (back[:experts].astype(F32) + back[experts:].astype(F32)).astype(BF16)
        dx = dx.reshape(experts * ROWS, dx.shape[2])
        term = jnp.dot(pick.astype(BF16), dx, preferred_element_type=F32)
        total = term if total is None else total + term
    out_ref[...] = total.astype(BF16)


def collect(experts, ids, back):
    tok = ids.shape[0]
    peers, _, half = back[0].shape
    cols = half
    whole = pl.BlockSpec((peers, ROWS, cols), lambda i: (0, 0, 0))
    return pl.pallas_call(
        lambda *refs: collect_kernel(experts, *refs),
        grid=(2,),
        in_specs=[pl.BlockSpec((tok, 2), lambda i: (0, 0)), whole, whole],
        out_specs=pl.BlockSpec((tok, cols), lambda i: (0, i)),
        out_shape=jax.ShapeDtypeStruct((tok, 2 * half), BF16),
        compiler_params=params(48),
        cost_estimate=pl.CostEstimate(
            flops=2 * 4 * tok * experts * ROWS * half, bytes_accessed=5 * MIB, transcendentals=0
        ),
        name="collect",
    )(ids, back[0], back[1])


def exchange(rows):
    return lax.all_to_all(rows, PEERS, split_axis=0, concat_axis=0, tiled=True)


def other_core(rows):
    return lax.ppermute(rows, "core", [(0, 1), (1, 0)])


def shards(tokens, grad_out, gates, expert_ids, w_gate, w_up, w_down):
    experts = lax.axis_size(EXPERT)
    wg, wu, wd = w_gate[0], w_up[0], w_down[0]
    got = []
    for chunk in range(2):
        got.append(exchange(pack(chunk, experts, expert_ids, gates, tokens, grad_out)))
    groups, back = [], []
    for chunk in range(2):
        mine = rows_pass(got[chunk], wg, wu, wd)
        theirs = rows_pass(other_core(got[chunk]), wg, wu, wd)
        groups += [mine[:5], theirs[:5]]
        partial = mine[5].astype(F32) + other_core(theirs[5]).astype(F32)
        back.append(exchange(partial.astype(BF16)))
    grads = weight_grads(groups)
    grad_tokens = collect(experts, expert_ids, back)
    return (grad_tokens,) + tuple(grad[None] for grad in grads)


def solution(mesh):
    fine = Mesh(mesh.devices.reshape(2, 2, 4, 4, 2), DEVICE)
    per_token = P(DEVICE, None)
    columns = P(EXPERT, None, ("yhi", "core"))
    rows = P(EXPERT, ("yhi", "core"), None)
    return jax.shard_map(
        shards,
        mesh=fine,
        in_specs=(per_token,) * 4 + (columns, columns, rows),
        out_specs=(per_token, columns, columns, rows),
        check_vma=False,
    )
```

```python
import jax
import jax.numpy as jnp
from jax import lax
from jax.experimental import pallas as pl
from jax.experimental.pallas import tpu as pltpu
from jax.sharding import Mesh, PartitionSpec as P

DEVICE = ("yhi", "core", "x", "z", "ylo")
EXPERT = ("x", "z", "ylo")
PEERS = ("yhi", "x", "z", "ylo")

BF16 = jnp.bfloat16
F32 = jnp.float32
RANKS = 8
ROWS = 2 * RANKS
MIB = 1024 * 1024

CONTRACT_LAST = (((1,), (1,)), ((), ()))
CONTRACT_ROWS = (((0,), (0,)), ((), ()))


def params(mib):
    return pltpu.CompilerParams(vmem_limit_bytes=mib * MIB)


def route_slots(ids_ref, experts, chunk):
    tok = ids_ref.shape[1]
    expert = lax.broadcasted_iota(jnp.int32, (experts, tok), 0)
    picks = [(ids_ref[k : k + 1, :] == expert).astype(F32) for k in range(2)]
    before = lax.broadcasted_iota(jnp.int32, (tok, tok), 0) < lax.broadcasted_iota(
        jnp.int32, (tok, tok), 1
    )
    ahead = jnp.dot(
        (picks[0] + picks[1]).astype(BF16), before.astype(BF16), preferred_element_type=F32
    )
    slots = []
    for k in range(2):
        rank = jnp.sum(ahead * picks[k], axis=0, keepdims=True).astype(jnp.int32) - chunk * RANKS
        inside = (rank >= 0) & (rank < RANKS)
        slots.append(jnp.where(inside, ids_ref[k : k + 1, :] * ROWS + rank, -1))
    return slots


def as_column(row):
    size = row.shape[1]
    same = lax.broadcasted_iota(jnp.int32, (size, size), 0) == lax.broadcasted_iota(
        jnp.int32, (size, size), 1
    )
    return jnp.sum(jnp.where(same, row, jnp.zeros_like(row)), axis=1, keepdims=True)


def pack_kernel(chunk, experts, ids_ref, gates_ref, tok_ref, grad_ref, out_ref, picks):
    tok = ids_ref.shape[1]

    @pl.when(pl.program_id(0) == 0)
    def _():
        slots = route_slots(ids_ref, experts, chunk)
        at = lax.broadcasted_iota(jnp.int32, (experts * ROWS, tok), 0)
        picks[0] = ((at == slots[0]) | (at == slots[1])).astype(BF16)
        for k in range(2):
            there = jnp.where(slots[k] >= 0, slots[k] + RANKS, -1)
            picks[1 + k] = (at == there).astype(BF16)

    packed = jnp.dot(picks[0], tok_ref[...], preferred_element_type=F32)
    for k in range(2):
        gate = as_column(gates_ref[k : k + 1, :])
        dy = (gate * grad_ref[...].astype(F32)).astype(BF16)
        packed = packed + jnp.dot(picks[1 + k], dy, preferred_element_type=F32)
    packed = packed.astype(BF16).reshape(experts, ROWS, packed.shape[1])
    out_ref[:experts] = packed
    out_ref[experts:] = packed


def pack(chunk, experts, ids, gates, tokens, grad_out):
    tok, width = tokens.shape
    cols = 512
    return pl.pallas_call(
        lambda *refs: pack_kernel(chunk, experts, *refs),
        grid=(width // cols,),
        in_specs=[
            pl.BlockSpec((2, tok), lambda i: (0, 0)),
            pl.BlockSpec((2, tok), lambda i: (0, 0)),
            pl.BlockSpec((tok, cols), lambda i: (0, i)),
            pl.BlockSpec((tok, cols), lambda i: (0, i)),
        ],
        out_specs=pl.BlockSpec((2 * experts, ROWS, cols), lambda i: (0, 0, i)),
        out_shape=jax.ShapeDtypeStruct((2 * experts, ROWS, width), BF16),
        scratch_shapes=[pltpu.VMEM((3, experts * ROWS, tok), BF16)],
        compiler_params=params(60),
        cost_estimate=cost(2 * 3 * tok * experts * ROWS * width, 12, 0),
        name="pack",
    )(ids, gates, tokens, grad_out)


def block(size, index):
    return pl.ds(index * size if isinstance(index, int) else pl.multiple_of(index * size, size), size)


def cost(flops, mib, transcendentals=0):
    return pl.CostEstimate(
        flops=flops // 8, bytes_accessed=mib * MIB // 8, transcendentals=transcendentals // 8
    )


def hidden_kernel(
    got0, got1, wg, wu, wd, x, dy, h, dg, du, dx,
    got_v, wg_v, wu_v, wd_v, x_v, dy_v, h_v, dg_v, du_v, dx_v,
    got_sem, w_sem, row_sem, hid_sem, dx_sem,
):
    peers, _, width = got0.shape
    hid = wg.shape[1]
    rows = peers * RANKS
    split, unit, out = 512, 256, 256
    splits, units = width // split, hid // unit

    def got_copy(group, i):
        return pltpu.make_async_copy(
            (got0, got1)[group].at[:, :, block(split, i)],
            got_v.at[group, :, :, block(split, i)],
            got_sem.at[group, i],
        )

    def w_copy(which, j):
        src, dst = ((wg, wg_v), (wu, wu_v), (wd, wd_v))[which]
        at = (block(unit, j), slice(None)) if which == 2 else (slice(None), block(unit, j))
        return pltpu.make_async_copy(src.at[at], dst.at[at], w_sem.at[which, j])

    def out_copy(src, dst, sem, group, cols, i):
        at = (block(rows, group), block(cols, i))
        return pltpu.make_async_copy(src.at[at], dst.at[at], sem)

    for i in range(splits):
        got_copy(0, i).start()
    for which in range(3):
        w_copy(which, 0).start()
    for i in range(splits):
        got_copy(1, i).start()
    for j in range(1, units):
        for which in range(3):
            w_copy(which, j).start()

    def row_copies(group, i):
        return [
            out_copy(src, dst, row_sem.at[n, group, i], group, split, i)
            for n, (src, dst) in enumerate(((x_v, x), (dy_v, dy)))
        ]

    def hid_copies(group, j):
        return [
            out_copy(src, dst, hid_sem.at[n, group, j], group, unit, j)
            for n, (src, dst) in enumerate(((h_v, h), (dg_v, dg), (du_v, du)))
        ]

    for group in range(2):
        here = block(rows, group)

        @pl.loop(0, splits)
        def _(i):
            got_copy(group, i).wait()
            cols = block(split, i)
            both = got_v[group, :, :, cols].astype(F32)
            x_v[here, cols] = both[:, :RANKS].reshape(rows, split).astype(BF16)
            dy_v[here, cols] = both[:, RANKS:].reshape(rows, split).astype(BF16)
            for copy in row_copies(group, i):
                copy.start()

        @pl.loop(0, units)
        def _(j):
            if group == 0:
                for which in range(3):
                    w_copy(which, j).wait()
            cols = block(unit, j)
            g = jnp.dot(x_v[here, :], wg_v[:, cols], preferred_element_type=F32)
            u = jnp.dot(x_v[here, :], wu_v[:, cols], preferred_element_type=F32)
            sig = jax.nn.sigmoid(g)
            silu = g * sig
            h_v[here, cols] = (silu * u).astype(BF16)
            slope = u * sig * (1.0 + g * (1.0 - sig))
            dh = lax.dot_general(
                dy_v[here, :], wd_v[cols, :], CONTRACT_LAST, preferred_element_type=F32
            )
            dg_v[here, cols] = (dh * slope).astype(BF16)
            du_v[here, cols] = (dh * silu).astype(BF16)
            for copy in hid_copies(group, j):
                copy.start()

        if group == 0:
            input_grad_tiles(dg_v, du_v, wg_v, wu_v, rows, out, dx_v)
            pltpu.make_async_copy(dx_v, dx, dx_sem).start()
    pltpu.make_async_copy(dx_v, dx, dx_sem).wait()
    for group in range(2):
        for copy in [c for i in range(splits) for c in row_copies(group, i)]:
            copy.wait()
        for copy in [c for j in range(units) for c in hid_copies(group, j)]:
            copy.wait()


def input_grad_tiles(dg, du, wg, wu, rows, cols, dx):
    peers = rows // RANKS
    half = wg.shape[0] // 2

    @pl.loop(0, half // cols)
    def _(i):
        parts = []
        for side in range(2):
            at = pl.ds(pl.multiple_of(side * half + i * cols, cols), cols)
            part = lax.dot_general(
                dg[:rows, :], wg[at, :], CONTRACT_LAST, preferred_element_type=F32
            ) + lax.dot_general(du[:rows, :], wu[at, :], CONTRACT_LAST, preferred_element_type=F32)
            parts.append(part.reshape(peers, RANKS, cols))
        dx[:, :, block(cols, i)] = jnp.concatenate(parts, axis=1).astype(BF16)


def hidden_pass(got0, got1, wg, wu, wd):
    peers, _, width = got0.shape
    hid = wg.shape[1]
    rows = 2 * peers * RANKS
    splits, units = width // 512, hid // 256
    wide, narrow = (jax.ShapeDtypeStruct((rows, n), BF16) for n in (width, hid))
    return pl.pallas_call(
        hidden_kernel,
        in_specs=[pl.BlockSpec(memory_space=pl.ANY)] * 5,
        out_specs=[pl.BlockSpec(memory_space=pl.ANY)] * 6,
        out_shape=[
            wide,
            wide,
            narrow,
            narrow,
            narrow,
            jax.ShapeDtypeStruct((peers, ROWS, width // 2), BF16),
        ],
        scratch_shapes=[
            pltpu.VMEM((2, peers, ROWS, width), BF16),
            pltpu.VMEM((width, hid), BF16),
            pltpu.VMEM((width, hid), BF16),
            pltpu.VMEM((hid, width), BF16),
            pltpu.VMEM((rows, width), BF16),
            pltpu.VMEM((rows, width), BF16),
            pltpu.VMEM((rows, hid), BF16),
            pltpu.VMEM((rows, hid), BF16),
            pltpu.VMEM((rows, hid), BF16),
            pltpu.VMEM((peers, ROWS, width // 2), BF16),
            pltpu.SemaphoreType.DMA((2, splits)),
            pltpu.SemaphoreType.DMA((3, units)),
            pltpu.SemaphoreType.DMA((2, 2, splits)),
            pltpu.SemaphoreType.DMA((3, 2, units)),
            pltpu.SemaphoreType.DMA,
        ],
        compiler_params=params(60),
        cost_estimate=cost(2 * 4 * rows * width * hid, 36, rows * hid),
        name="hidden",
    )(got0, got1, wg, wu, wd)


def input_grad_kernel(dg_ref, du_ref, wg0_ref, wg1_ref, wu0_ref, wu1_ref, more_ref, dx_ref):
    peers, _, cols = dx_ref.shape
    parts = []
    for wg_ref, wu_ref in ((wg0_ref, wu0_ref), (wg1_ref, wu1_ref)):
        part = lax.dot_general(
            dg_ref[...], wg_ref[...], CONTRACT_LAST, preferred_element_type=F32
        ) + lax.dot_general(du_ref[...], wu_ref[...], CONTRACT_LAST, preferred_element_type=F32)
        parts.append(part.reshape(peers, RANKS, cols))
    dx_ref[...] = (jnp.concatenate(parts, axis=1) + more_ref[...].astype(F32)).astype(BF16)


def input_grad(dg, du, wg, wu, more):
    hid = dg.shape[1]
    width = wg.shape[0]
    peers = more.shape[0]
    rows = peers * RANKS
    cols = 256
    steps = width // 2 // cols
    whole = pl.BlockSpec((rows, hid), lambda i: (1, 0))
    low = pl.BlockSpec((cols, hid), lambda i: (i, 0))
    high = pl.BlockSpec((cols, hid), lambda i: (i + steps, 0))
    out = pl.BlockSpec((peers, ROWS, cols), lambda i: (0, 0, i))
    return pl.pallas_call(
        input_grad_kernel,
        grid=(steps,),
        in_specs=[whole, whole, low, high, low, high, out],
        out_specs=out,
        out_shape=jax.ShapeDtypeStruct(more.shape, BF16),
        compiler_params=params(60),
        cost_estimate=cost(2 * 2 * rows * width * hid, 14, 0),
        name="input_grad",
    )(dg, du, wg, wg, wu, wu, more)


def down_grad_kernel(dy_ref, h_ref, *refs):
    total = lax.dot_general(dy_ref[...], h_ref[...], CONTRACT_ROWS, preferred_element_type=F32)
    if len(refs) > 1:
        total = (refs[0][...] + total).T
    refs[-1][...] = total.astype(refs[-1].dtype)


def down_grad(dy, h, before=None):
    rows, width = dy.shape
    hid = h.shape[1]
    cols = 512
    tall = pl.BlockSpec((cols, hid), lambda i: (i, 0))
    more = () if before is None else (before,)
    return pl.pallas_call(
        down_grad_kernel,
        grid=(width // cols,),
        in_specs=[
            pl.BlockSpec((rows, cols), lambda i: (0, i)),
            pl.BlockSpec((rows, hid), lambda i: (0, 0)),
        ]
        + [tall] * len(more),
        out_specs=pl.BlockSpec((hid, cols), lambda i: (0, i)) if more else tall,
        out_shape=jax.ShapeDtypeStruct(
            (hid, width) if more else (width, hid), BF16 if more else F32
        ),
        compiler_params=params(60),
        cost_estimate=cost(2 * rows * width * hid, 20, 0),
        name="down_grad",
    )(dy, h, *more)


def gate_up_kernel(x0_ref, x1_ref, dg0_ref, dg1_ref, du0_ref, du1_ref, gate_ref, up_ref):
    def write(left, right, out_ref):
        total = lax.dot_general(
            x0_ref[...], left[...], CONTRACT_ROWS, preferred_element_type=F32
        ) + lax.dot_general(x1_ref[...], right[...], CONTRACT_ROWS, preferred_element_type=F32)
        out_ref[...] = total.astype(BF16)

    pl.when(pl.program_id(0) == 0)(lambda: write(dg0_ref, dg1_ref, gate_ref))
    pl.when(pl.program_id(0) == 1)(lambda: write(du0_ref, du1_ref, up_ref))


def gate_up_grads(x, dg, du):
    rows, width = x[0].shape
    hid = dg[0].shape[1]
    cols = 512
    steps = width // cols
    x_spec = pl.BlockSpec((rows, cols), lambda o, i: (0, i))
    whole = pl.BlockSpec((rows, hid), lambda o, i: (0, 0))
    flat = jax.ShapeDtypeStruct((width, hid), BF16)
    return pl.pallas_call(
        gate_up_kernel,
        grid=(2, steps),
        in_specs=[x_spec] * 2 + [whole] * 4,
        out_specs=[
            pl.BlockSpec((cols, hid), lambda o, i: (jnp.where(o == 0, i, steps - 1), 0)),
            pl.BlockSpec((cols, hid), lambda o, i: (jnp.where(o == 0, 0, i), 0)),
        ],
        out_shape=[flat, flat],
        compiler_params=params(60),
        cost_estimate=cost(2 * 4 * rows * width * hid, 32, 0),
        name="gate_up_grads",
    )(*x, *dg, *du)


def collect_kernel(chunk, experts, ids_ref, back_ref, *refs):
    half = pl.program_id(0)
    tok = ids_ref.shape[1]
    lane = lax.broadcasted_iota(jnp.int32, (tok, experts * ROWS), 1)
    pick = jnp.zeros((tok, experts * ROWS), jnp.bool_)
    for slot in route_slots(ids_ref, experts, chunk):
        there = jnp.where(slot >= 0, slot + half * RANKS, -1)
        pick = pick | (lane == as_column(there))
    dx = (back_ref[:experts].astype(F32) + back_ref[experts:].astype(F32)).astype(BF16)
    dx = dx.reshape(experts * ROWS, dx.shape[2])
    total = jnp.dot(pick.astype(BF16), dx, preferred_element_type=F32)
    if len(refs) > 1:
        total = refs[0][...] + total
    refs[-1][...] = total.astype(refs[-1].dtype)


def collect(chunk, experts, ids, back, before=None):
    tok = ids.shape[1]
    peers, _, half = back.shape
    out = pl.BlockSpec((tok, half), lambda i: (0, i))
    more = () if before is None else (before,)
    return pl.pallas_call(
        lambda *refs: collect_kernel(chunk, experts, *refs),
        grid=(2,),
        in_specs=[
            pl.BlockSpec((2, tok), lambda i: (0, 0)),
            pl.BlockSpec((peers, ROWS, half), lambda i: (0, 0, 0)),
        ]
        + [out] * len(more),
        out_specs=out,
        out_shape=jax.ShapeDtypeStruct((tok, 2 * half), BF16 if more else F32),
        compiler_params=params(60),
        cost_estimate=cost(2 * 2 * tok * experts * ROWS * half, 4, 0),
        name="collect",
    )(ids, back, *more)


def exchange(rows):
    return lax.all_to_all(rows, PEERS, split_axis=0, concat_axis=0, tiled=True)


def other_core(rows):
    return lax.ppermute(rows, "core", [(0, 1), (1, 0)])


def shards(tokens, grad_out, gates, expert_ids, w_gate, w_up, w_down):
    experts = lax.axis_size(EXPERT)
    wg, wu, wd = w_gate[0], w_up[0], w_down[0]
    ids, scales = expert_ids.T, gates.T
    sends = [pack(chunk, experts, ids, scales, tokens, grad_out) for chunk in range(2)]
    got0, send1 = lax.optimization_barrier((exchange(sends[0]), sends[1]))
    got = [got0, exchange(send1)]
    x, dg, du, back, down, dx = [], [], [], [], None, None
    for chunk in range(2):
        rows = got[chunk]
        if chunk:
            rows, down, dx = lax.optimization_barrier((rows, down, dx))
        now = hidden_pass(other_core(rows), rows, wg, wu, wd)
        sent, dy, h = other_core(now[5]), now[1], now[2]
        if chunk:
            part = collect(0, experts, ids, back[0])
            dy, part = lax.optimization_barrier((dy, part))
        down = down_grad(dy, h, down)
        sent, down = lax.optimization_barrier((sent, down))
        dx = input_grad(now[3], now[4], wg, wu, sent)
        back.append(exchange(dx))
        for held, value in zip((x, dg, du), (now[0], now[3], now[4])):
            held.append(value)
    x[1], _ = lax.optimization_barrier((x[1], dx))
    grad_gate, grad_up = gate_up_grads(x, dg, du)
    grad_tokens = collect(1, experts, ids, back[1], part)
    return (grad_tokens, grad_gate[None], grad_up[None], down[None])


def solution(mesh):
    fine = Mesh(mesh.devices.reshape(2, 2, 4, 4, 2), DEVICE)
    per_token = P(DEVICE, None)
    columns = P(EXPERT, None, ("yhi", "core"))
    rows = P(EXPERT, ("yhi", "core"), None)
    return jax.shard_map(
        shards,
        mesh=fine,
        in_specs=(per_token,) * 4 + (columns, columns, rows),
        out_specs=(per_token, columns, columns, rows),
        check_vma=False,
    )
```

```python
import jax
import jax.numpy as jnp
from jax import lax
from jax.experimental import pallas as pl
from jax.experimental.pallas import tpu as pltpu
from jax.sharding import Mesh, PartitionSpec as P

DEVICE = ("yhi", "core", "x", "z", "ylo")
EXPERT = ("x", "z", "ylo")
PEERS = ("yhi", "x", "z", "ylo")

BF16 = jnp.bfloat16
F32 = jnp.float32
RANKS = 8
ROWS = 2 * RANKS
MIB = 1024 * 1024

CONTRACT_LAST = (((1,), (1,)), ((), ()))
CONTRACT_ROWS = (((0,), (0,)), ((), ()))


def params(mib):
    return pltpu.CompilerParams(vmem_limit_bytes=mib * MIB)


def route_slots(ids_ref, experts, chunk):
    tok = ids_ref.shape[1]
    expert = lax.broadcasted_iota(jnp.int32, (experts, tok), 0)
    picks = [(ids_ref[k : k + 1, :] == expert).astype(F32) for k in range(2)]
    before = lax.broadcasted_iota(jnp.int32, (tok, tok), 0) < lax.broadcasted_iota(
        jnp.int32, (tok, tok), 1
    )
    ahead = jnp.dot(
        (picks[0] + picks[1]).astype(BF16), before.astype(BF16), preferred_element_type=F32
    )
    slots = []
    for k in range(2):
        rank = jnp.sum(ahead * picks[k], axis=0, keepdims=True).astype(jnp.int32) - chunk * RANKS
        inside = (rank >= 0) & (rank < RANKS)
        slots.append(jnp.where(inside, ids_ref[k : k + 1, :] * ROWS + rank, -1))
    return slots


def as_column(row):
    size = row.shape[1]
    same = lax.broadcasted_iota(jnp.int32, (size, size), 0) == lax.broadcasted_iota(
        jnp.int32, (size, size), 1
    )
    return jnp.sum(jnp.where(same, row, jnp.zeros_like(row)), axis=1, keepdims=True)


def pack_kernel(chunk, experts, ids_ref, gates_ref, tok_ref, grad_ref, out_ref, picks):
    tok = ids_ref.shape[1]

    @pl.when(pl.program_id(0) == 0)
    def _():
        slots = route_slots(ids_ref, experts, chunk)
        at = lax.broadcasted_iota(jnp.int32, (experts * ROWS, tok), 0)
        picks[0] = ((at == slots[0]) | (at == slots[1])).astype(BF16)
        for k in range(2):
            there = jnp.where(slots[k] >= 0, slots[k] + RANKS, -1)
            picks[1 + k] = (at == there).astype(BF16)

    packed = jnp.dot(picks[0], tok_ref[...], preferred_element_type=F32)
    for k in range(2):
        gate = as_column(gates_ref[k : k + 1, :])
        dy = (gate * grad_ref[...].astype(F32)).astype(BF16)
        packed = packed + jnp.dot(picks[1 + k], dy, preferred_element_type=F32)
    packed = packed.astype(BF16).reshape(experts, ROWS, packed.shape[1])
    out_ref[:experts] = packed
    out_ref[experts:] = packed


def pack(chunk, experts, ids, gates, tokens, grad_out):
    tok, width = tokens.shape
    cols = 512
    return pl.pallas_call(
        lambda *refs: pack_kernel(chunk, experts, *refs),
        grid=(width // cols,),
        in_specs=[
            pl.BlockSpec((2, tok), lambda i: (0, 0)),
            pl.BlockSpec((2, tok), lambda i: (0, 0)),
            pl.BlockSpec((tok, cols), lambda i: (0, i)),
            pl.BlockSpec((tok, cols), lambda i: (0, i)),
        ],
        out_specs=pl.BlockSpec((2 * experts, ROWS, cols), lambda i: (0, 0, i)),
        out_shape=jax.ShapeDtypeStruct((2 * experts, ROWS, width), BF16),
        scratch_shapes=[pltpu.VMEM((3, experts * ROWS, tok), BF16)],
        compiler_params=params(60),
        cost_estimate=cost(2 * 3 * tok * experts * ROWS * width, 12, 0),
        name="pack",
    )(ids, gates, tokens, grad_out)


def block(size, index):
    return pl.ds(index * size if isinstance(index, int) else pl.multiple_of(index * size, size), size)


def cost(flops, mib, transcendentals=0):
    return pl.CostEstimate(
        flops=flops // 8, bytes_accessed=mib * MIB // 8, transcendentals=transcendentals // 8
    )


def hidden_kernel(
    unit, out, got0, got1, wg, wu, wd, x, dy, h, dg, du, dx0, dx1,
    got_v0, got_v1, wg_v, wu_v, wd_v, x_v0, x_v1, dy_v0, dy_v1, h_v, dg_v, du_v, dx_v,
    got_sem, w_sem, row_sem, hid_sem, dx_sem,
):
    got, got_v = (got0, got1), (got_v0, got_v1)
    x_v, dy_v = (x_v0, x_v1), (dy_v0, dy_v1)
    peers, _, width = got0.shape
    hid = wg.shape[1]
    rows = peers * RANKS
    split = 512
    splits, units = width // split, hid // unit

    def got_copy(group, i):
        at = (slice(None), slice(None), block(split, i))
        return pltpu.make_async_copy(
            got[group].at[at], got_v[group].at[at], got_sem.at[group, i]
        )

    def w_copy(which, j):
        src, dst = ((wg, wg_v), (wu, wu_v), (wd, wd_v))[which]
        at = (block(unit, j), slice(None)) if which == 2 else (slice(None), block(unit, j))
        return pltpu.make_async_copy(src.at[at], dst.at[at], w_sem.at[which, j])

    def row_copies(group):
        at = (block(rows, group), slice(None))
        return [
            pltpu.make_async_copy(src[group], dst.at[at], row_sem.at[n, group])
            for n, (src, dst) in enumerate(((x_v, x), (dy_v, dy)))
        ]

    hid_copies = [
        pltpu.make_async_copy(src, dst, hid_sem.at[n])
        for n, (src, dst) in enumerate(((h_v, h), (dg_v, dg), (du_v, du)))
    ]
    dx_copies = [
        pltpu.make_async_copy(dx_v.at[block(peers, n)], (dx0, dx1)[n], dx_sem.at[n])
        for n in range(2)
    ]

    for i in range(splits):
        got_copy(0, i).start()
    for which in range(3):
        w_copy(which, 0).start()
    for i in range(splits):
        got_copy(1, i).start()
    for j in range(1, units):
        for which in range(3):
            w_copy(which, j).start()

    def split_rows(group, i):
        cols = block(split, i)
        both = got_v[group][:, :, cols].astype(F32)
        x_v[group][:, cols] = both[:, :RANKS].reshape(rows, split).astype(BF16)
        dy_v[group][:, cols] = both[:, RANKS:].reshape(rows, split).astype(BF16)

    @pl.loop(0, splits)
    def _(i):
        got_copy(0, i).wait()
        split_rows(0, i)

    for group in range(2):
        here = block(rows, group)

        @pl.loop(0, units)
        def _(j):
            if group == 0:
                for which in range(3):
                    w_copy(which, j).wait()
                for part in range(splits // units):
                    got_copy(1, j * (splits // units) + part).wait()
                for part in range(splits // units):
                    split_rows(1, j * (splits // units) + part)
            cols = block(unit, j)
            g = jnp.dot(x_v[group][...], wg_v[:, cols], preferred_element_type=F32)
            u = jnp.dot(x_v[group][...], wu_v[:, cols], preferred_element_type=F32)
            sig = jax.nn.sigmoid(g)
            silu = g * sig
            h_v[here, cols] = (silu * u).astype(BF16)
            slope = u * sig * (1.0 + g * (1.0 - sig))
            dh = lax.dot_general(
                dy_v[group][...], wd_v[cols, :], CONTRACT_LAST, preferred_element_type=F32
            )
            dg_v[here, cols] = (dh * slope).astype(BF16)
            du_v[here, cols] = (dh * silu).astype(BF16)

        for copy in row_copies(group):
            copy.start()
    for copy in hid_copies:
        copy.start()

    half = width // 2

    @pl.loop(0, half // out)
    def _(i):
        parts = []
        for side in range(2):
            at = block(out, side * (half // out) + i)
            part = lax.dot_general(
                dg_v[...], wg_v[at, :], CONTRACT_LAST, preferred_element_type=F32
            ) + lax.dot_general(du_v[...], wu_v[at, :], CONTRACT_LAST, preferred_element_type=F32)
            parts.append(part.reshape(2 * peers, RANKS, out))
        dx_v[:, :, block(out, i)] = jnp.concatenate(parts, axis=1).astype(BF16)

    for copy in dx_copies:
        copy.start()
    for copy in [c for group in range(2) for c in row_copies(group)] + hid_copies + dx_copies:
        copy.wait()


def hidden_pass(got0, got1, wg, wu, wd, unit=512, out=512):
    peers, _, width = got0.shape
    hid = wg.shape[1]
    rows = 2 * peers * RANKS
    splits, units = width // 512, hid // unit
    wide, narrow = (jax.ShapeDtypeStruct((rows, n), BF16) for n in (width, hid))
    dx = jax.ShapeDtypeStruct((peers, ROWS, width // 2), BF16)
    return pl.pallas_call(
        lambda *refs: hidden_kernel(unit, out, *refs),
        in_specs=[pl.BlockSpec(memory_space=pl.ANY)] * 5,
        out_specs=[pl.BlockSpec(memory_space=pl.ANY)] * 7,
        out_shape=[wide, wide, narrow, narrow, narrow, dx, dx],
        scratch_shapes=[
            pltpu.VMEM((peers, ROWS, width), BF16),
            pltpu.VMEM((peers, ROWS, width), BF16),
            pltpu.VMEM((width, hid), BF16),
            pltpu.VMEM((width, hid), BF16),
            pltpu.VMEM((hid, width), BF16),
            pltpu.VMEM((rows // 2, width), BF16),
            pltpu.VMEM((rows // 2, width), BF16),
            pltpu.VMEM((rows // 2, width), BF16),
            pltpu.VMEM((rows // 2, width), BF16),
            pltpu.VMEM((rows, hid), BF16),
            pltpu.VMEM((rows, hid), BF16),
            pltpu.VMEM((rows, hid), BF16),
            pltpu.VMEM((2 * peers, ROWS, width // 2), BF16),
            pltpu.SemaphoreType.DMA((2, splits)),
            pltpu.SemaphoreType.DMA((3, units)),
            pltpu.SemaphoreType.DMA((2, 2)),
            pltpu.SemaphoreType.DMA((3,)),
            pltpu.SemaphoreType.DMA((2,)),
        ],
        compiler_params=params(60),
        cost_estimate=cost(2 * 5 * rows * width * hid, 36, rows * hid),
        name="hidden",
    )(got0, got1, wg, wu, wd)


def add_kernel(a_ref, b_ref, out_ref):
    out_ref[...] = (a_ref[...].astype(F32) + b_ref[...].astype(F32)).astype(BF16)


def add(a, b):
    peers, rows, width = a.shape
    part = pl.BlockSpec((peers // 4, rows, width), lambda i: (i, 0, 0))
    return pl.pallas_call(
        add_kernel,
        grid=(4,),
        in_specs=[part, part],
        out_specs=part,
        out_shape=jax.ShapeDtypeStruct(a.shape, BF16),
        compiler_params=params(32),
        cost_estimate=cost(0, 6, 0),
        name="add",
    )(a, b)


def early_grads_kernel(x_ref, dy_ref, dg_ref, h_ref, gate_ref, down_ref):
    for left, right, out in ((x_ref, dg_ref, gate_ref), (dy_ref, h_ref, down_ref)):
        out[...] = lax.dot_general(
            left[...], right[...], CONTRACT_ROWS, preferred_element_type=F32
        )


def early_grads(x, dy, dg, h):
    rows, width = dy.shape
    hid = h.shape[1]
    cols = 512
    narrow = pl.BlockSpec((rows, cols), lambda i: (0, i))
    whole = pl.BlockSpec((rows, hid), lambda i: (0, 0))
    tall = pl.BlockSpec((cols, hid), lambda i: (i, 0))
    return pl.pallas_call(
        early_grads_kernel,
        grid=(width // cols,),
        in_specs=[narrow, narrow, whole, whole],
        out_specs=[tall, tall],
        out_shape=[jax.ShapeDtypeStruct((width, hid), F32)] * 2,
        compiler_params=params(60),
        cost_estimate=cost(2 * 2 * rows * width * hid, 28, 0),
        name="early_grads",
    )(x, dy, dg, h)


def weight_grads_kernel(
    x0_ref, x1_ref, dy_ref, gate0_ref, down0_ref, dg1, du0, du1, h1, gate_ref, up_ref, down_ref,
    dg1_v, du0_v, du1_v, h1_v, sem,
):
    whole = ((dg1, dg1_v), (du0, du0_v), (du1, du1_v), (h1, h1_v))
    copies = [pltpu.make_async_copy(src, dst, sem.at[n]) for n, (src, dst) in enumerate(whole)]
    first = pl.program_id(0) == 0

    @pl.when(first)
    def _():
        for copy in copies:
            copy.start()

    def arrived(*numbers):
        @pl.when(first)
        def _():
            for n in numbers:
                copies[n].wait()

    def term(left, right):
        return lax.dot_general(
            left[...], right[...], CONTRACT_ROWS, preferred_element_type=F32
        )

    arrived(0)
    gate_ref[...] = (gate0_ref[...] + term(x1_ref, dg1_v)).astype(BF16)
    arrived(1, 2)
    up_ref[...] = (term(x0_ref, du0_v) + term(x1_ref, du1_v)).astype(BF16)
    arrived(3)
    down_ref[...] = (down0_ref[...] + term(dy_ref, h1_v)).T.astype(BF16)


def weight_grads(x, du, dg1, dy1, h1, early):
    rows, width = dy1.shape
    hid = h1.shape[1]
    cols = 512
    narrow = pl.BlockSpec((rows, cols), lambda i: (0, i))
    tall = pl.BlockSpec((cols, hid), lambda i: (i, 0))
    flat = jax.ShapeDtypeStruct((width, hid), BF16)
    return pl.pallas_call(
        weight_grads_kernel,
        grid=(width // cols,),
        in_specs=[narrow] * 3 + [tall] * 2 + [pl.BlockSpec(memory_space=pl.ANY)] * 4,
        out_specs=[tall, tall, pl.BlockSpec((hid, cols), lambda i: (0, i))],
        out_shape=[flat, flat, jax.ShapeDtypeStruct((hid, width), BF16)],
        scratch_shapes=[pltpu.VMEM((rows, hid), BF16)] * 4 + [pltpu.SemaphoreType.DMA((4,))],
        compiler_params=params(60),
        cost_estimate=cost(2 * 4 * rows * width * hid, 48, 0),
        name="weight_grads",
    )(*x, dy1, *early, dg1, *du, h1)


def collect_kernel(chunk, experts, ids_ref, back_ref, *refs):
    half = pl.program_id(0)
    tok = ids_ref.shape[1]
    lane = lax.broadcasted_iota(jnp.int32, (tok, experts * ROWS), 1)
    pick = jnp.zeros((tok, experts * ROWS), jnp.bool_)
    for slot in route_slots(ids_ref, experts, chunk):
        there = jnp.where(slot >= 0, slot + half * RANKS, -1)
        pick = pick | (lane == as_column(there))
    dx = (back_ref[:experts].astype(F32) + back_ref[experts:].astype(F32)).astype(BF16)
    dx = dx.reshape(experts * ROWS, dx.shape[2])
    total = jnp.dot(pick.astype(BF16), dx, preferred_element_type=F32)
    if len(refs) > 1:
        total = refs[0][...] + total
    refs[-1][...] = total.astype(refs[-1].dtype)


def collect(chunk, experts, ids, back, before=None):
    tok = ids.shape[1]
    peers, _, half = back.shape
    out = pl.BlockSpec((tok, half), lambda i: (0, i))
    more = () if before is None else (before,)
    return pl.pallas_call(
        lambda *refs: collect_kernel(chunk, experts, *refs),
        grid=(2,),
        in_specs=[
            pl.BlockSpec((2, tok), lambda i: (0, 0)),
            pl.BlockSpec((peers, ROWS, half), lambda i: (0, 0, 0)),
        ]
        + [out] * len(more),
        out_specs=out,
        out_shape=jax.ShapeDtypeStruct((tok, 2 * half), BF16 if more else F32),
        compiler_params=params(24),
        cost_estimate=cost(2 * 2 * tok * experts * ROWS * half, 4, 0),
        name="collect",
    )(ids, back, *more)


def exchange(rows):
    return lax.all_to_all(rows, PEERS, split_axis=0, concat_axis=0, tiled=True)


def other_core(rows):
    return lax.ppermute(rows, "core", [(0, 1), (1, 0)])


def shards(tokens, grad_out, gates, expert_ids, w_gate, w_up, w_down):
    experts = lax.axis_size(EXPERT)
    wg, wu, wd = w_gate[0], w_up[0], w_down[0]
    ids, scales = expert_ids.T, gates.T
    sends = [pack(chunk, experts, ids, scales, tokens, grad_out) for chunk in range(2)]
    got0, send1 = lax.optimization_barrier((exchange(sends[0]), sends[1]))
    got = [got0, exchange(send1)]
    x, du, back = [], [], []
    for chunk in range(2):
        rows = got[chunk]
        if chunk:
            rows, early, dx = lax.optimization_barrier((rows, early, dx))
        now = hidden_pass(other_core(rows), rows, wg, wu, wd)
        x.append(now[0])
        du.append(now[4])
        theirs = now[5]
        if chunk:
            first, theirs = lax.optimization_barrier((back[0], theirs))
            part = collect(0, experts, ids, first)
        sent = other_core(theirs)
        if chunk:
            sent, part = lax.optimization_barrier((sent, part))
        else:
            early = early_grads(now[0], now[1], now[3], now[2])
            sent, early = lax.optimization_barrier((sent, early))
        dx = add(now[6], sent)
        back.append(exchange(dx))
    x[1], _ = lax.optimization_barrier((x[1], dx))
    grad_gate, grad_up, down = weight_grads(x, du, now[3], now[1], now[2], early)
    grad_tokens = collect(1, experts, ids, back[1], part)
    return (grad_tokens, grad_gate[None], grad_up[None], down[None])


def solution(mesh):
    fine = Mesh(mesh.devices.reshape(2, 2, 4, 4, 2), DEVICE)
    per_token = P(DEVICE, None)
    columns = P(EXPERT, None, ("yhi", "core"))
    rows = P(EXPERT, ("yhi", "core"), None)
    return jax.shard_map(
        shards,
        mesh=fine,
        in_specs=(per_token,) * 4 + (columns, columns, rows),
        out_specs=(per_token, columns, columns, rows),
        check_vma=False,
    )
```

```python
import jax
import jax.numpy as jnp
from jax import lax
from jax.experimental import pallas as pl
from jax.experimental.pallas import tpu as pltpu
from jax.sharding import Mesh, PartitionSpec as P

DEVICE = ("yhi", "core", "x", "z", "ylo")
EXPERT = ("x", "z", "ylo")
PEERS = ("yhi", "x", "z", "ylo")

BF16 = jnp.bfloat16
F32 = jnp.float32
RANKS = 8
ROWS = 2 * RANKS
MIB = 1024 * 1024

CONTRACT_LAST = (((1,), (1,)), ((), ()))
CONTRACT_ROWS = (((0,), (0,)), ((), ()))


def params(mib):
    return pltpu.CompilerParams(vmem_limit_bytes=mib * MIB)


def route_slots(ids_ref, experts, chunk):
    tok = ids_ref.shape[1]
    expert = lax.broadcasted_iota(jnp.int32, (experts, tok), 0)
    picks = [(ids_ref[k : k + 1, :] == expert).astype(F32) for k in range(2)]
    before = lax.broadcasted_iota(jnp.int32, (tok, tok), 0) < lax.broadcasted_iota(
        jnp.int32, (tok, tok), 1
    )
    ahead = jnp.dot(
        (picks[0] + picks[1]).astype(BF16), before.astype(BF16), preferred_element_type=F32
    )
    slots = []
    for k in range(2):
        rank = jnp.sum(ahead * picks[k], axis=0, keepdims=True).astype(jnp.int32) - chunk * RANKS
        inside = (rank >= 0) & (rank < RANKS)
        slots.append(jnp.where(inside, ids_ref[k : k + 1, :] * ROWS + rank, -1))
    return slots


def as_column(row):
    size = row.shape[1]
    same = lax.broadcasted_iota(jnp.int32, (size, size), 0) == lax.broadcasted_iota(
        jnp.int32, (size, size), 1
    )
    return jnp.sum(jnp.where(same, row, jnp.zeros_like(row)), axis=1, keepdims=True)


def pack_kernel(chunk, experts, ids_ref, gates_ref, tok_ref, grad_ref, out_ref, picks, gates):
    tok = ids_ref.shape[1]

    @pl.when(pl.program_id(0) == 0)
    def _():
        slots = route_slots(ids_ref, experts, chunk)
        at = lax.broadcasted_iota(jnp.int32, (experts * ROWS, tok), 0)
        picks[0] = ((at == slots[0]) | (at == slots[1])).astype(BF16)
        for k in range(2):
            there = jnp.where(slots[k] >= 0, slots[k] + RANKS, -1)
            picks[1 + k] = (at == there).astype(BF16)
            gates[k] = as_column(gates_ref[k : k + 1, :])

    packed = jnp.dot(picks[0], tok_ref[...], preferred_element_type=F32)
    for k in range(2):
        dy = (gates[k] * grad_ref[...].astype(F32)).astype(BF16)
        packed = packed + jnp.dot(picks[1 + k], dy, preferred_element_type=F32)
    packed = packed.astype(BF16).reshape(experts, ROWS, packed.shape[1])
    out_ref[:experts] = packed
    out_ref[experts:] = packed


def pack(chunk, experts, ids, gates, tokens, grad_out, cols=1024):
    tok, width = tokens.shape
    return pl.pallas_call(
        lambda *refs: pack_kernel(chunk, experts, *refs),
        grid=(width // cols,),
        in_specs=[
            pl.BlockSpec((2, tok), lambda i: (0, 0)),
            pl.BlockSpec((2, tok), lambda i: (0, 0)),
            pl.BlockSpec((tok, cols), lambda i: (0, i)),
            pl.BlockSpec((tok, cols), lambda i: (0, i)),
        ],
        out_specs=pl.BlockSpec((2 * experts, ROWS, cols), lambda i: (0, 0, i)),
        out_shape=jax.ShapeDtypeStruct((2 * experts, ROWS, width), BF16),
        scratch_shapes=[
            pltpu.VMEM((3, experts * ROWS, tok), BF16),
            pltpu.VMEM((2, tok, 1), F32),
        ],
        compiler_params=params(60),
        cost_estimate=cost(2 * 3 * tok * experts * ROWS * width, 12, 0),
        name="pack",
    )(ids, gates, tokens, grad_out)


def block(size, index):
    return pl.ds(index * size if isinstance(index, int) else pl.multiple_of(index * size, size), size)


def cost(flops, mib, transcendentals=0):
    return pl.CostEstimate(
        flops=flops // 8, bytes_accessed=mib * MIB // 8, transcendentals=transcendentals // 8
    )


def hidden_kernel(
    got0, got1, wg, wu, wd, x, dy, h, dg, du, dx0, dx1,
    got_v0, got_v1, wg_v, wu_v, wd_v, x_v0, x_v1, dy_v0, dy_v1, h_v, dg_v, du_v, dx_v,
    got_sem, w_sem, row_sem, hid_sem, dx_sem,
):
    got, got_v = (got0, got1), (got_v0, got_v1)
    x_v, dy_v = (x_v0, x_v1), (dy_v0, dy_v1)
    peers, _, width = got0.shape
    hid = wg.shape[1]
    rows = peers * RANKS
    split, out, unit = 512, 512, 256
    splits, units = width // split, hid // unit

    def got_copy(group, i):
        at = (slice(None), slice(None), block(split, i))
        return pltpu.make_async_copy(
            got[group].at[at], got_v[group].at[at], got_sem.at[group, i]
        )

    def w_copy(which, j):
        src, dst = ((wg, wg_v), (wu, wu_v), (wd, wd_v))[which]
        at = (block(unit, j), slice(None)) if which == 2 else (slice(None), block(unit, j))
        return pltpu.make_async_copy(src.at[at], dst.at[at], w_sem.at[which, j])

    def row_copies(group):
        at = (block(rows, group), slice(None))
        return [
            pltpu.make_async_copy(src[group], dst.at[at], row_sem.at[n, group])
            for n, (src, dst) in enumerate(((x_v, x), (dy_v, dy)))
        ]

    def hid_copies(group):
        at = (block(rows, group), slice(None))
        return [
            pltpu.make_async_copy(src.at[at], dst.at[at], hid_sem.at[n, group])
            for n, (src, dst) in enumerate(((h_v, h), (dg_v, dg), (du_v, du)))
        ]

    def dx_copies(i):
        cols = block(out, i)
        return [
            pltpu.make_async_copy(
                dx_v.at[block(peers, n), :, cols], dx.at[:, :, cols], dx_sem.at[n, i]
            )
            for n, dx in enumerate((dx0, dx1))
        ]

    for i in range(splits):
        got_copy(0, i).start()
    for j in range(units):
        if j == 2:
            for i in range(splits):
                got_copy(1, i).start()
        for which in range(3):
            w_copy(which, j).start()

    def split_rows(group, i):
        cols = block(split, i)
        both = got_v[group][:, :, cols].astype(F32)
        x_v[group][:, cols] = both[:, :RANKS].reshape(rows, split).astype(BF16)
        dy_v[group][:, cols] = both[:, RANKS:].reshape(rows, split).astype(BF16)

    @pl.loop(0, splits)
    def _(i):
        got_copy(0, i).wait()
        split_rows(0, i)

    wide = 2 * unit
    for group in range(2):
        here = block(rows, group)

        @pl.loop(0, hid // wide)
        def _(j):
            if group == 0:
                for part in range(2):
                    for which in range(3):
                        w_copy(which, 2 * j + part).wait()
            cols = block(wide, j)
            g = jnp.dot(x_v[group][...], wg_v[:, cols], preferred_element_type=F32)
            u = jnp.dot(x_v[group][...], wu_v[:, cols], preferred_element_type=F32)
            sig = jax.nn.sigmoid(g)
            silu = g * sig
            h_v[here, cols] = (silu * u).astype(BF16)
            slope = u * sig * (1.0 + g * (1.0 - sig))
            dh = lax.dot_general(
                dy_v[group][...], wd_v[cols, :], CONTRACT_LAST, preferred_element_type=F32
            )
            dg_v[here, cols] = (dh * slope).astype(BF16)
            du_v[here, cols] = (dh * silu).astype(BF16)

        for copy in row_copies(group) + hid_copies(group):
            copy.start()
        if group == 0:

            @pl.loop(0, splits)
            def _(i):
                got_copy(1, i).wait()
                split_rows(1, i)

    half = width // 2

    @pl.loop(0, half // out)
    def _(i):
        parts = []
        for side in range(2):
            at = block(out, side * (half // out) + i)
            part = lax.dot_general(
                dg_v[...], wg_v[at, :], CONTRACT_LAST, preferred_element_type=F32
            ) + lax.dot_general(du_v[...], wu_v[at, :], CONTRACT_LAST, preferred_element_type=F32)
            parts.append(part.reshape(2 * peers, RANKS, out))
        dx_v[:, :, block(out, i)] = jnp.concatenate(parts, axis=1).astype(BF16)
        for copy in dx_copies(i):
            copy.start()

    for copy in [c for group in range(2) for c in row_copies(group) + hid_copies(group)]:
        copy.wait()
    for copy in [c for i in range(half // out) for c in dx_copies(i)]:
        copy.wait()


def hidden_pass(got0, got1, wg, wu, wd):
    peers, _, width = got0.shape
    hid = wg.shape[1]
    rows = 2 * peers * RANKS
    splits, units = width // 512, hid // 256
    wide, narrow = (jax.ShapeDtypeStruct((rows, n), BF16) for n in (width, hid))
    dx = jax.ShapeDtypeStruct((peers, ROWS, width // 2), BF16)
    return pl.pallas_call(
        hidden_kernel,
        in_specs=[pl.BlockSpec(memory_space=pl.ANY)] * 5,
        out_specs=[pl.BlockSpec(memory_space=pl.ANY)] * 7,
        out_shape=[wide, wide, narrow, narrow, narrow, dx, dx],
        scratch_shapes=[
            pltpu.VMEM((peers, ROWS, width), BF16),
            pltpu.VMEM((peers, ROWS, width), BF16),
            pltpu.VMEM((width, hid), BF16),
            pltpu.VMEM((width, hid), BF16),
            pltpu.VMEM((hid, width), BF16),
            pltpu.VMEM((rows // 2, width), BF16),
            pltpu.VMEM((rows // 2, width), BF16),
            pltpu.VMEM((rows // 2, width), BF16),
            pltpu.VMEM((rows // 2, width), BF16),
            pltpu.VMEM((rows, hid), BF16),
            pltpu.VMEM((rows, hid), BF16),
            pltpu.VMEM((rows, hid), BF16),
            pltpu.VMEM((2 * peers, ROWS, width // 2), BF16),
            pltpu.SemaphoreType.DMA((2, splits)),
            pltpu.SemaphoreType.DMA((3, units)),
            pltpu.SemaphoreType.DMA((2, 2)),
            pltpu.SemaphoreType.DMA((3, 2)),
            pltpu.SemaphoreType.DMA((2, width // 1024)),
        ],
        compiler_params=params(60),
        cost_estimate=cost(2 * 5 * rows * width * hid, 36, rows * hid),
        name="hidden",
    )(got0, got1, wg, wu, wd)


def add_kernel(a_ref, b_ref, out_ref, sums, sem):
    parts = sem.shape[0]
    size = sums.shape[0] // parts
    copies = []
    for n in range(parts):
        at = block(size, n)
        sums[at] = (a_ref[at].astype(F32) + b_ref[at].astype(F32)).astype(BF16)
        copies.append(pltpu.make_async_copy(sums.at[at], out_ref.at[at], sem.at[n]))
        copies[-1].start()
    for copy in copies:
        copy.wait()


def add(a, b):
    return pl.pallas_call(
        add_kernel,
        in_specs=[pl.BlockSpec(memory_space=pltpu.VMEM)] * 2,
        out_specs=pl.BlockSpec(memory_space=pl.ANY),
        out_shape=jax.ShapeDtypeStruct(a.shape, BF16),
        scratch_shapes=[pltpu.VMEM(a.shape, BF16), pltpu.SemaphoreType.DMA((4,))],
        compiler_params=params(32),
        cost_estimate=cost(0, 6, 0),
        name="add",
    )(a, b)


def early_grads_kernel(x_ref, dy_ref, dg_ref, h_ref, gate_ref, down_ref):
    for left, right, out in ((x_ref, dg_ref, gate_ref), (dy_ref, h_ref, down_ref)):
        out[...] = lax.dot_general(
            left[...], right[...], CONTRACT_ROWS, preferred_element_type=F32
        )


def early_grads(x, dy, dg, h):
    rows, width = dy.shape
    hid = h.shape[1]
    cols = 512
    narrow = pl.BlockSpec((rows, cols), lambda i: (0, i))
    whole = pl.BlockSpec((rows, hid), lambda i: (0, 0))
    tall = pl.BlockSpec((cols, hid), lambda i: (i, 0))
    return pl.pallas_call(
        early_grads_kernel,
        grid=(width // cols,),
        in_specs=[narrow, narrow, whole, whole],
        out_specs=[tall, tall],
        out_shape=[jax.ShapeDtypeStruct((width, hid), F32)] * 2,
        compiler_params=params(60),
        cost_estimate=cost(2 * 2 * rows * width * hid, 28, 0),
        name="early_grads",
    )(x, dy, dg, h)


def weight_grads_kernel(
    x0_ref, x1_ref, dy_ref, gate0_ref, down0_ref, dg1, du0, du1, h1, gate_ref, up_ref, down_ref,
    dg1_v, du0_v, du1_v, h1_v, sem,
):
    whole = ((dg1, dg1_v), (du0, du0_v), (du1, du1_v), (h1, h1_v))
    copies = [pltpu.make_async_copy(src, dst, sem.at[n]) for n, (src, dst) in enumerate(whole)]
    first = pl.program_id(0) == 0

    @pl.when(first)
    def _():
        for copy in copies:
            copy.start()

    def arrived(*numbers):
        @pl.when(first)
        def _():
            for n in numbers:
                copies[n].wait()

    def term(left, right):
        return lax.dot_general(
            left[...], right[...], CONTRACT_ROWS, preferred_element_type=F32
        )

    arrived(0)
    gate_ref[...] = (gate0_ref[...] + term(x1_ref, dg1_v)).astype(BF16)
    arrived(1, 2)
    up_ref[...] = (term(x0_ref, du0_v) + term(x1_ref, du1_v)).astype(BF16)
    arrived(3)
    down_ref[...] = (down0_ref[...] + term(dy_ref, h1_v)).T.astype(BF16)


def weight_grads(x, du, dg1, dy1, h1, early):
    rows, width = dy1.shape
    hid = h1.shape[1]
    cols = 512
    narrow = pl.BlockSpec((rows, cols), lambda i: (0, i))
    tall = pl.BlockSpec((cols, hid), lambda i: (i, 0))
    flat = jax.ShapeDtypeStruct((width, hid), BF16)
    return pl.pallas_call(
        weight_grads_kernel,
        grid=(width // cols,),
        in_specs=[narrow] * 3 + [tall] * 2 + [pl.BlockSpec(memory_space=pl.ANY)] * 4,
        out_specs=[tall, tall, pl.BlockSpec((hid, cols), lambda i: (0, i))],
        out_shape=[flat, flat, jax.ShapeDtypeStruct((hid, width), BF16)],
        scratch_shapes=[pltpu.VMEM((rows, hid), BF16)] * 4 + [pltpu.SemaphoreType.DMA((4,))],
        compiler_params=params(60),
        cost_estimate=cost(2 * 4 * rows * width * hid, 48, 0),
        name="weight_grads",
    )(*x, dy1, *early, dg1, *du, h1)


def collect_kernel(chunk, experts, ids_ref, back_ref, *refs):
    half = pl.program_id(0)
    tok = ids_ref.shape[1]
    lane = lax.broadcasted_iota(jnp.int32, (tok, experts * ROWS), 1)
    pick = jnp.zeros((tok, experts * ROWS), jnp.bool_)
    for slot in route_slots(ids_ref, experts, chunk):
        there = jnp.where(slot >= 0, slot + half * RANKS, -1)
        pick = pick | (lane == as_column(there))
    dx = (back_ref[:experts].astype(F32) + back_ref[experts:].astype(F32)).astype(BF16)
    dx = dx.reshape(experts * ROWS, dx.shape[2])
    total = jnp.dot(pick.astype(BF16), dx, preferred_element_type=F32)
    if len(refs) > 1:
        total = refs[0][...] + total
    refs[-1][...] = total.astype(refs[-1].dtype)


def collect(chunk, experts, ids, back, before=None):
    tok = ids.shape[1]
    peers, _, half = back.shape
    out = pl.BlockSpec((tok, half), lambda i: (0, i))
    more = () if before is None else (before,)
    return pl.pallas_call(
        lambda *refs: collect_kernel(chunk, experts, *refs),
        grid=(2,),
        in_specs=[
            pl.BlockSpec((2, tok), lambda i: (0, 0)),
            pl.BlockSpec((peers, ROWS, half), lambda i: (0, 0, 0)),
        ]
        + [out] * len(more),
        out_specs=out,
        out_shape=jax.ShapeDtypeStruct((tok, 2 * half), BF16 if more else F32),
        compiler_params=params(24),
        cost_estimate=cost(2 * 2 * tok * experts * ROWS * half, 4, 0),
        name="collect",
    )(ids, back, *more)


def exchange(rows):
    return lax.all_to_all(rows, PEERS, split_axis=0, concat_axis=0, tiled=True)


def other_core(rows):
    return lax.ppermute(rows, "core", [(0, 1), (1, 0)])


def shards(tokens, grad_out, gates, expert_ids, w_gate, w_up, w_down):
    experts = lax.axis_size(EXPERT)
    wg, wu, wd = w_gate[0], w_up[0], w_down[0]
    ids, scales = expert_ids.T, gates.T
    sends = [pack(chunk, experts, ids, scales, tokens, grad_out) for chunk in range(2)]
    got0, send1 = lax.optimization_barrier((exchange(sends[0]), sends[1]))
    got = [got0, exchange(send1)]
    x, du, back = [], [], []
    for chunk in range(2):
        rows = got[chunk]
        if chunk:
            rows, early, dx = lax.optimization_barrier((rows, early, dx))
        now = hidden_pass(other_core(rows), rows, wg, wu, wd)
        x.append(now[0])
        du.append(now[4])
        theirs = now[5]
        if chunk:
            first, theirs = lax.optimization_barrier((back[0], theirs))
            part = collect(0, experts, ids, first)
        sent = other_core(theirs)
        if chunk:
            sent, part = lax.optimization_barrier((sent, part))
        else:
            early = early_grads(now[0], now[1], now[3], now[2])
            sent, early = lax.optimization_barrier((sent, early))
        dx = add(now[6], sent)
        back.append(exchange(dx))
    x[1], _ = lax.optimization_barrier((x[1], dx))
    grad_gate, grad_up, down = weight_grads(x, du, now[3], now[1], now[2], early)
    grad_tokens = collect(1, experts, ids, back[1], part)
    return (grad_tokens, grad_gate[None], grad_up[None], down[None])


def solution(mesh):
    fine = Mesh(mesh.devices.reshape(2, 2, 4, 4, 2), DEVICE)
    per_token = P(DEVICE, None)
    columns = P(EXPERT, None, ("yhi", "core"))
    rows = P(EXPERT, ("yhi", "core"), None)
    return jax.shard_map(
        shards,
        mesh=fine,
        in_specs=(per_token,) * 4 + (columns, columns, rows),
        out_specs=(per_token, columns, columns, rows),
        check_vma=False,
    )
```

```python
import jax
import jax.numpy as jnp
from jax import lax
from jax.experimental import pallas as pl
from jax.experimental.pallas import tpu as pltpu
from jax.sharding import Mesh, PartitionSpec as P

DEVICE = ("yhi", "core", "x", "z", "ylo")
EXPERT = ("x", "z", "ylo")
PEERS = ("yhi", "x", "z", "ylo")

BF16 = jnp.bfloat16
F32 = jnp.float32
RANKS = 8
ROWS = 2 * RANKS
MIB = 1024 * 1024

CONTRACT_LAST = (((1,), (1,)), ((), ()))
CONTRACT_ROWS = (((0,), (0,)), ((), ()))


def params(mib):
    return pltpu.CompilerParams(vmem_limit_bytes=mib * MIB)


def route_slots(ids_ref, experts, chunk):
    tok = ids_ref.shape[1]
    expert = lax.broadcasted_iota(jnp.int32, (experts, tok), 0)
    picks = [(ids_ref[k : k + 1, :] == expert).astype(F32) for k in range(2)]
    before = lax.broadcasted_iota(jnp.int32, (tok, tok), 0) < lax.broadcasted_iota(
        jnp.int32, (tok, tok), 1
    )
    ahead = jnp.dot(
        (picks[0] + picks[1]).astype(BF16), before.astype(BF16), preferred_element_type=F32
    )
    slots = []
    for k in range(2):
        rank = jnp.sum(ahead * picks[k], axis=0, keepdims=True).astype(jnp.int32) - chunk * RANKS
        inside = (rank >= 0) & (rank < RANKS)
        slots.append(jnp.where(inside, ids_ref[k : k + 1, :] * ROWS + rank, -1))
    return slots


def as_column(row):
    size = row.shape[1]
    same = lax.broadcasted_iota(jnp.int32, (size, size), 0) == lax.broadcasted_iota(
        jnp.int32, (size, size), 1
    )
    return jnp.sum(jnp.where(same, row, jnp.zeros_like(row)), axis=1, keepdims=True)


def pack_kernel(chunk, experts, ids_ref, gates_ref, tok_ref, grad_ref, out, pick, rows, packed, sem):
    tok, width = tok_ref.shape
    cols = 512
    slots = route_slots(ids_ref, experts, chunk)
    at = lax.broadcasted_iota(jnp.int32, (experts * ROWS, tok), 0)
    pick[:, :tok] = ((at == slots[0]) | (at == slots[1])).astype(BF16)
    rows[:tok] = tok_ref[...]
    for k in range(2):
        here = slice((1 + k) * tok, (2 + k) * tok)
        there = jnp.where(slots[k] >= 0, slots[k] + RANKS, -1)
        pick[:, here] = (at == there).astype(BF16)
        gate = as_column(gates_ref[k : k + 1, :])
        rows[here] = (gate * grad_ref[...].astype(F32)).astype(BF16)

    copies = []
    for i in range(width // cols):
        part = block(cols, i)
        packed[:, :, part] = (
            jnp.dot(pick[...], rows[:, part], preferred_element_type=F32)
            .astype(BF16)
            .reshape(experts, ROWS, cols)
        )
        for yhi in range(2):
            copies.append(
                pltpu.make_async_copy(
                    packed.at[:, :, part], out.at[block(experts, yhi), :, part], sem.at[yhi, i]
                )
            )
            copies[-1].start()
    for copy in copies:
        copy.wait()


def pack(chunk, experts, ids, gates, tokens, grad_out):
    tok, width = tokens.shape
    return pl.pallas_call(
        lambda *refs: pack_kernel(chunk, experts, *refs),
        in_specs=[pl.BlockSpec(memory_space=pltpu.VMEM)] * 4,
        out_specs=pl.BlockSpec(memory_space=pl.ANY),
        out_shape=jax.ShapeDtypeStruct((2 * experts, ROWS, width), BF16),
        scratch_shapes=[
            pltpu.VMEM((experts * ROWS, 3 * tok), BF16),
            pltpu.VMEM((3 * tok, width), BF16),
            pltpu.VMEM((experts, ROWS, width), BF16),
            pltpu.SemaphoreType.DMA((2, width // 512)),
        ],
        compiler_params=params(60),
        cost_estimate=cost(2 * 3 * tok * experts * ROWS * width, 12, 0),
        name="pack",
    )(ids, gates, tokens, grad_out)


def block(size, index):
    return pl.ds(index * size if isinstance(index, int) else pl.multiple_of(index * size, size), size)


def cost(flops, mib, transcendentals=0):
    return pl.CostEstimate(
        flops=flops // 8, bytes_accessed=mib * MIB // 8, transcendentals=transcendentals // 8
    )


def hidden_kernel(
    got0, got1, wg, wu, wd, x, dy, h, dg, du, dx0, dx1,
    got_v0, got_v1, wg_v, wu_v, wd_v, x_v0, x_v1, dy_v0, dy_v1, h_v, dg_v, du_v, dx_v,
    got_sem, w_sem, row_sem, hid_sem, dx_sem,
):
    got, got_v = (got0, got1), (got_v0, got_v1)
    x_v, dy_v = (x_v0, x_v1), (dy_v0, dy_v1)
    peers, _, width = got0.shape
    hid = wg.shape[1]
    rows = peers * RANKS
    split, out, unit = 512, 512, 256
    splits, units = width // split, hid // unit

    def got_copy(group, i):
        at = (slice(None), slice(None), block(split, i))
        return pltpu.make_async_copy(
            got[group].at[at], got_v[group].at[at], got_sem.at[group, i]
        )

    def w_copy(which, j):
        src, dst = ((wg, wg_v), (wu, wu_v), (wd, wd_v))[which]
        at = (block(unit, j), slice(None)) if which == 2 else (slice(None), block(unit, j))
        return pltpu.make_async_copy(src.at[at], dst.at[at], w_sem.at[which, j])

    def row_copies(group):
        at = (block(rows, group), slice(None))
        return [
            pltpu.make_async_copy(src[group], dst.at[at], row_sem.at[n, group])
            for n, (src, dst) in enumerate(((x_v, x), (dy_v, dy)))
        ]

    def hid_copies(group):
        at = (block(rows, group), slice(None))
        return [
            pltpu.make_async_copy(src.at[at], dst.at[at], hid_sem.at[n, group])
            for n, (src, dst) in enumerate(((h_v, h), (dg_v, dg), (du_v, du)))
        ]

    def dx_copies(i):
        cols = block(out, i)
        return [
            pltpu.make_async_copy(
                dx_v.at[block(peers, n), :, cols], dx.at[:, :, cols], dx_sem.at[n, i]
            )
            for n, dx in enumerate((dx0, dx1))
        ]

    for i in range(splits):
        got_copy(0, i).start()
    for j in range(units):
        if j == 2:
            for i in range(splits):
                got_copy(1, i).start()
        for which in range(3):
            w_copy(which, j).start()

    def split_rows(group, i):
        cols = block(split, i)
        both = got_v[group][:, :, cols].astype(F32)
        x_v[group][:, cols] = both[:, :RANKS].reshape(rows, split).astype(BF16)
        dy_v[group][:, cols] = both[:, RANKS:].reshape(rows, split).astype(BF16)

    @pl.loop(0, splits)
    def _(i):
        got_copy(0, i).wait()
        split_rows(0, i)

    wide = 2 * unit
    for group in range(2):
        here = block(rows, group)

        @pl.loop(0, hid // wide)
        def _(j):
            if group == 0:
                for part in range(2):
                    for which in range(3):
                        w_copy(which, 2 * j + part).wait()
            cols = block(wide, j)
            g = jnp.dot(x_v[group][...], wg_v[:, cols], preferred_element_type=F32)
            u = jnp.dot(x_v[group][...], wu_v[:, cols], preferred_element_type=F32)
            sig = jax.nn.sigmoid(g)
            silu = g * sig
            h_v[here, cols] = (silu * u).astype(BF16)
            slope = u * sig * (1.0 + g * (1.0 - sig))
            dh = lax.dot_general(
                dy_v[group][...], wd_v[cols, :], CONTRACT_LAST, preferred_element_type=F32
            )
            dg_v[here, cols] = (dh * slope).astype(BF16)
            du_v[here, cols] = (dh * silu).astype(BF16)

        for copy in row_copies(group) + hid_copies(group):
            copy.start()
        if group == 0:

            @pl.loop(0, splits)
            def _(i):
                got_copy(1, i).wait()
                split_rows(1, i)

    half = width // 2

    @pl.loop(0, half // out)
    def _(i):
        parts = []
        for side in range(2):
            at = block(out, side * (half // out) + i)
            part = lax.dot_general(
                dg_v[...], wg_v[at, :], CONTRACT_LAST, preferred_element_type=F32
            ) + lax.dot_general(du_v[...], wu_v[at, :], CONTRACT_LAST, preferred_element_type=F32)
            parts.append(part.reshape(2 * peers, RANKS, out))
        dx_v[:, :, block(out, i)] = jnp.concatenate(parts, axis=1).astype(BF16)
        for copy in dx_copies(i):
            copy.start()

    for copy in [c for group in range(2) for c in row_copies(group) + hid_copies(group)]:
        copy.wait()
    for copy in [c for i in range(half // out) for c in dx_copies(i)]:
        copy.wait()


def hidden_pass(got0, got1, wg, wu, wd):
    peers, _, width = got0.shape
    hid = wg.shape[1]
    rows = 2 * peers * RANKS
    splits, units = width // 512, hid // 256
    wide, narrow = (jax.ShapeDtypeStruct((rows, n), BF16) for n in (width, hid))
    dx = jax.ShapeDtypeStruct((peers, ROWS, width // 2), BF16)
    return pl.pallas_call(
        hidden_kernel,
        in_specs=[pl.BlockSpec(memory_space=pl.ANY)] * 5,
        out_specs=[pl.BlockSpec(memory_space=pl.ANY)] * 7,
        out_shape=[wide, wide, narrow, narrow, narrow, dx, dx],
        scratch_shapes=[
            pltpu.VMEM((peers, ROWS, width), BF16),
            pltpu.VMEM((peers, ROWS, width), BF16),
            pltpu.VMEM((width, hid), BF16),
            pltpu.VMEM((width, hid), BF16),
            pltpu.VMEM((hid, width), BF16),
            pltpu.VMEM((rows // 2, width), BF16),
            pltpu.VMEM((rows // 2, width), BF16),
            pltpu.VMEM((rows // 2, width), BF16),
            pltpu.VMEM((rows // 2, width), BF16),
            pltpu.VMEM((rows, hid), BF16),
            pltpu.VMEM((rows, hid), BF16),
            pltpu.VMEM((rows, hid), BF16),
            pltpu.VMEM((2 * peers, ROWS, width // 2), BF16),
            pltpu.SemaphoreType.DMA((2, splits)),
            pltpu.SemaphoreType.DMA((3, units)),
            pltpu.SemaphoreType.DMA((2, 2)),
            pltpu.SemaphoreType.DMA((3, 2)),
            pltpu.SemaphoreType.DMA((2, width // 1024)),
        ],
        compiler_params=params(60),
        cost_estimate=cost(2 * 5 * rows * width * hid, 36, rows * hid),
        name="hidden",
    )(got0, got1, wg, wu, wd)


def add_kernel(a_ref, b_ref, out_ref, sums, sem):
    parts = sem.shape[0]
    size = sums.shape[0] // parts
    copies = []
    for n in range(parts):
        at = block(size, n)
        sums[at] = (a_ref[at].astype(F32) + b_ref[at].astype(F32)).astype(BF16)
        copies.append(pltpu.make_async_copy(sums.at[at], out_ref.at[at], sem.at[n]))
        copies[-1].start()
    for copy in copies:
        copy.wait()


def add(a, b):
    return pl.pallas_call(
        add_kernel,
        in_specs=[pl.BlockSpec(memory_space=pltpu.VMEM)] * 2,
        out_specs=pl.BlockSpec(memory_space=pl.ANY),
        out_shape=jax.ShapeDtypeStruct(a.shape, BF16),
        scratch_shapes=[pltpu.VMEM(a.shape, BF16), pltpu.SemaphoreType.DMA((4,))],
        compiler_params=params(32),
        cost_estimate=cost(0, 6, 0),
        name="add",
    )(a, b)


def early_grads_kernel(x_ref, dy_ref, dg_ref, h_ref, gate_ref, down_ref):
    for left, right, out in ((x_ref, dg_ref, gate_ref), (dy_ref, h_ref, down_ref)):
        out[...] = lax.dot_general(
            left[...], right[...], CONTRACT_ROWS, preferred_element_type=F32
        )


def early_grads(x, dy, dg, h):
    rows, width = dy.shape
    hid = h.shape[1]
    cols = 512
    narrow = pl.BlockSpec((rows, cols), lambda i: (0, i))
    whole = pl.BlockSpec((rows, hid), lambda i: (0, 0))
    tall = pl.BlockSpec((cols, hid), lambda i: (i, 0))
    return pl.pallas_call(
        early_grads_kernel,
        grid=(width // cols,),
        in_specs=[narrow, narrow, whole, whole],
        out_specs=[tall, tall],
        out_shape=[jax.ShapeDtypeStruct((width, hid), F32)] * 2,
        compiler_params=params(60),
        cost_estimate=cost(2 * 2 * rows * width * hid, 28, 0),
        name="early_grads",
    )(x, dy, dg, h)


def weight_grads_kernel(
    x0_ref, x1_ref, dy_ref, gate0_ref, down0_ref, dg1, du0, du1, h1, gate_ref, up_ref, down_ref,
    dg1_v, du0_v, du1_v, h1_v, sem,
):
    whole = ((dg1, dg1_v), (du0, du0_v), (du1, du1_v), (h1, h1_v))
    copies = [pltpu.make_async_copy(src, dst, sem.at[n]) for n, (src, dst) in enumerate(whole)]
    first = pl.program_id(0) == 0

    @pl.when(first)
    def _():
        for copy in copies:
            copy.start()

    def arrived(*numbers):
        @pl.when(first)
        def _():
            for n in numbers:
                copies[n].wait()

    def term(left, right):
        return lax.dot_general(
            left[...], right[...], CONTRACT_ROWS, preferred_element_type=F32
        )

    arrived(0)
    gate_ref[...] = (gate0_ref[...] + term(x1_ref, dg1_v)).astype(BF16)
    arrived(1, 2)
    up_ref[...] = (term(x0_ref, du0_v) + term(x1_ref, du1_v)).astype(BF16)
    arrived(3)
    down_ref[...] = (down0_ref[...] + term(dy_ref, h1_v)).T.astype(BF16)


def weight_grads(x, du, dg1, dy1, h1, early):
    rows, width = dy1.shape
    hid = h1.shape[1]
    cols = 512
    narrow = pl.BlockSpec((rows, cols), lambda i: (0, i))
    tall = pl.BlockSpec((cols, hid), lambda i: (i, 0))
    flat = jax.ShapeDtypeStruct((width, hid), BF16)
    return pl.pallas_call(
        weight_grads_kernel,
        grid=(width // cols,),
        in_specs=[narrow] * 3 + [tall] * 2 + [pl.BlockSpec(memory_space=pl.ANY)] * 4,
        out_specs=[tall, tall, pl.BlockSpec((hid, cols), lambda i: (0, i))],
        out_shape=[flat, flat, jax.ShapeDtypeStruct((hid, width), BF16)],
        scratch_shapes=[pltpu.VMEM((rows, hid), BF16)] * 4 + [pltpu.SemaphoreType.DMA((4,))],
        compiler_params=params(60),
        cost_estimate=cost(2 * 4 * rows * width * hid, 48, 0),
        name="weight_grads",
    )(*x, dy1, *early, dg1, *du, h1)


def collect_kernel(chunk, experts, ids_ref, back_ref, *refs):
    half = pl.program_id(0)
    tok = ids_ref.shape[1]
    lane = lax.broadcasted_iota(jnp.int32, (tok, experts * ROWS), 1)
    pick = jnp.zeros((tok, experts * ROWS), jnp.bool_)
    for slot in route_slots(ids_ref, experts, chunk):
        there = jnp.where(slot >= 0, slot + half * RANKS, -1)
        pick = pick | (lane == as_column(there))
    dx = (back_ref[:experts].astype(F32) + back_ref[experts:].astype(F32)).astype(BF16)
    dx = dx.reshape(experts * ROWS, dx.shape[2])
    total = jnp.dot(pick.astype(BF16), dx, preferred_element_type=F32)
    if len(refs) > 1:
        total = refs[0][...] + total
    refs[-1][...] = total.astype(refs[-1].dtype)


def collect(chunk, experts, ids, back, before=None):
    tok = ids.shape[1]
    peers, _, half = back.shape
    out = pl.BlockSpec((tok, half), lambda i: (0, i))
    more = () if before is None else (before,)
    return pl.pallas_call(
        lambda *refs: collect_kernel(chunk, experts, *refs),
        grid=(2,),
        in_specs=[
            pl.BlockSpec((2, tok), lambda i: (0, 0)),
            pl.BlockSpec((peers, ROWS, half), lambda i: (0, 0, 0)),
        ]
        + [out] * len(more),
        out_specs=out,
        out_shape=jax.ShapeDtypeStruct((tok, 2 * half), BF16 if more else F32),
        compiler_params=params(24),
        cost_estimate=cost(2 * 2 * tok * experts * ROWS * half, 4, 0),
        name="collect",
    )(ids, back, *more)


def exchange(rows):
    return lax.all_to_all(rows, PEERS, split_axis=0, concat_axis=0, tiled=True)


def other_core(rows):
    return lax.ppermute(rows, "core", [(0, 1), (1, 0)])


def shards(tokens, grad_out, gates, expert_ids, w_gate, w_up, w_down):
    experts = lax.axis_size(EXPERT)
    wg, wu, wd = w_gate[0], w_up[0], w_down[0]
    ids, scales = expert_ids.T, gates.T
    sends = [pack(chunk, experts, ids, scales, tokens, grad_out) for chunk in range(2)]
    got0, send1 = lax.optimization_barrier((exchange(sends[0]), sends[1]))
    got = [got0, exchange(send1)]
    x, du, back = [], [], []
    for chunk in range(2):
        rows = got[chunk]
        if chunk:
            rows, early, dx = lax.optimization_barrier((rows, early, dx))
        now = hidden_pass(other_core(rows), rows, wg, wu, wd)
        x.append(now[0])
        du.append(now[4])
        theirs = now[5]
        if chunk:
            first, theirs = lax.optimization_barrier((back[0], theirs))
            part = collect(0, experts, ids, first)
        sent = other_core(theirs)
        if chunk:
            sent, part = lax.optimization_barrier((sent, part))
        else:
            early = early_grads(now[0], now[1], now[3], now[2])
            sent, early = lax.optimization_barrier((sent, early))
        dx = add(now[6], sent)
        back.append(exchange(dx))
    x[1], _ = lax.optimization_barrier((x[1], dx))
    grad_gate, grad_up, down = weight_grads(x, du, now[3], now[1], now[2], early)
    grad_tokens = collect(1, experts, ids, back[1], part)
    return (grad_tokens, grad_gate[None], grad_up[None], down[None])


def solution(mesh):
    fine = Mesh(mesh.devices.reshape(2, 2, 4, 4, 2), DEVICE)
    per_token = P(DEVICE, None)
    columns = P(EXPERT, None, ("yhi", "core"))
    rows = P(EXPERT, ("yhi", "core"), None)
    return jax.shard_map(
        shards,
        mesh=fine,
        in_specs=(per_token,) * 4 + (columns, columns, rows),
        out_specs=(per_token, columns, columns, rows),
        check_vma=False,
    )
```

```python
import jax
import jax.numpy as jnp
from jax import lax
from jax.experimental import pallas as pl
from jax.experimental.pallas import tpu as pltpu
from jax.sharding import Mesh, PartitionSpec as P

DEVICE = ("yhi", "core", "x", "z", "ylo")
EXPERT = ("x", "z", "ylo")
PEERS = ("yhi", "x", "z", "ylo")

BF16 = jnp.bfloat16
F32 = jnp.float32
RANKS = 8
ROWS = 2 * RANKS
MIB = 1024 * 1024

CONTRACT_LAST = (((1,), (1,)), ((), ()))
CONTRACT_ROWS = (((0,), (0,)), ((), ()))


def params(mib):
    return pltpu.CompilerParams(vmem_limit_bytes=mib * MIB)


def route_slots(ids_ref, experts, chunk):
    tok = ids_ref.shape[1]
    expert = lax.broadcasted_iota(jnp.int32, (experts, tok), 0)
    picks = [(ids_ref[k : k + 1, :] == expert).astype(F32) for k in range(2)]
    before = lax.broadcasted_iota(jnp.int32, (tok, tok), 0) < lax.broadcasted_iota(
        jnp.int32, (tok, tok), 1
    )
    ahead = jnp.dot(
        (picks[0] + picks[1]).astype(BF16), before.astype(BF16), preferred_element_type=F32
    )
    slots = []
    for k in range(2):
        rank = jnp.sum(ahead * picks[k], axis=0, keepdims=True).astype(jnp.int32) - chunk * RANKS
        inside = (rank >= 0) & (rank < RANKS)
        slots.append(jnp.where(inside, ids_ref[k : k + 1, :] * ROWS + rank, -1))
    return slots


def as_column(row):
    size = row.shape[1]
    same = lax.broadcasted_iota(jnp.int32, (size, size), 0) == lax.broadcasted_iota(
        jnp.int32, (size, size), 1
    )
    return jnp.sum(jnp.where(same, row, jnp.zeros_like(row)), axis=1, keepdims=True)


def pack_kernel(chunk, experts, ids_ref, gates_ref, tok_ref, grad_ref, out, pick, rows, packed, sem):
    tok, width = tok_ref.shape
    cols = 512
    slots = route_slots(ids_ref, experts, chunk)
    at = lax.broadcasted_iota(jnp.int32, (experts * ROWS, tok), 0)
    pick[:, :tok] = ((at == slots[0]) | (at == slots[1])).astype(BF16)
    rows[:tok] = tok_ref[...]
    for k in range(2):
        here = slice((1 + k) * tok, (2 + k) * tok)
        there = jnp.where(slots[k] >= 0, slots[k] + RANKS, -1)
        pick[:, here] = (at == there).astype(BF16)
        gate = as_column(gates_ref[k : k + 1, :])
        rows[here] = (gate * grad_ref[...].astype(F32)).astype(BF16)

    copies = []
    for i in range(width // cols):
        part = block(cols, i)
        packed[:, :, part] = (
            jnp.dot(pick[...], rows[:, part], preferred_element_type=F32)
            .astype(BF16)
            .reshape(experts, ROWS, cols)
        )
        for yhi in range(2):
            copies.append(
                pltpu.make_async_copy(
                    packed.at[:, :, part], out.at[block(experts, yhi), :, part], sem.at[yhi, i]
                )
            )
            copies[-1].start()
    for copy in copies:
        copy.wait()


def pack(chunk, experts, ids, gates, tokens, grad_out):
    tok, width = tokens.shape
    return pl.pallas_call(
        lambda *refs: pack_kernel(chunk, experts, *refs),
        in_specs=[pl.BlockSpec(memory_space=pltpu.VMEM)] * 4,
        out_specs=pl.BlockSpec(memory_space=pl.ANY),
        out_shape=jax.ShapeDtypeStruct((2 * experts, ROWS, width), BF16),
        scratch_shapes=[
            pltpu.VMEM((experts * ROWS, 3 * tok), BF16),
            pltpu.VMEM((3 * tok, width), BF16),
            pltpu.VMEM((experts, ROWS, width), BF16),
            pltpu.SemaphoreType.DMA((2, width // 512)),
        ],
        compiler_params=params(60),
        cost_estimate=cost(2 * 3 * tok * experts * ROWS * width, 12, 0),
        name="pack",
    )(ids, gates, tokens, grad_out)


def block(size, index):
    return pl.ds(index * size if isinstance(index, int) else pl.multiple_of(index * size, size), size)


def cost(flops, mib, transcendentals=0):
    return pl.CostEstimate(
        flops=flops // 8, bytes_accessed=mib * MIB // 8, transcendentals=transcendentals // 8
    )


def hidden_kernel(
    got0, got1, wg, wu, wd, x, dy, h, dg, du, dx0, dx1,
    got_v0, got_v1, wg_v, wu_v, wd_v, x_v0, x_v1, dy_v0, dy_v1, h_v, dg_v, du_v, dx_v,
    got_sem, w_sem, row_sem, hid_sem, dx_sem,
):
    got, got_v = (got0, got1), (got_v0, got_v1)
    x_v, dy_v = (x_v0, x_v1), (dy_v0, dy_v1)
    peers, _, width = got0.shape
    hid = wg.shape[1]
    rows = peers * RANKS
    split, out, unit = 512, 512, 256
    splits, units = width // split, hid // unit

    def got_copy(group, i):
        at = (slice(None), slice(None), block(split, i))
        return pltpu.make_async_copy(
            got[group].at[at], got_v[group].at[at], got_sem.at[group, i]
        )

    def w_copy(which, j):
        src, dst = ((wg, wg_v), (wu, wu_v), (wd, wd_v))[which]
        at = (block(unit, j), slice(None)) if which == 2 else (slice(None), block(unit, j))
        return pltpu.make_async_copy(src.at[at], dst.at[at], w_sem.at[which, j])

    def row_copies(group):
        at = (block(rows, group), slice(None))
        return [
            pltpu.make_async_copy(src[group], dst.at[at], row_sem.at[n, group])
            for n, (src, dst) in enumerate(((x_v, x), (dy_v, dy)))
        ]

    def hid_copies(group):
        at = (block(rows, group), slice(None))
        return [
            pltpu.make_async_copy(src.at[at], dst.at[at], hid_sem.at[n, group])
            for n, (src, dst) in enumerate(((h_v, h), (dg_v, dg), (du_v, du)))
        ]

    def dx_copies(i):
        cols = block(out, i)
        return [
            pltpu.make_async_copy(
                dx_v.at[block(peers, n), :, cols], dx.at[:, :, cols], dx_sem.at[n, i]
            )
            for n, dx in enumerate((dx0, dx1))
        ]

    for i in range(splits):
        got_copy(0, i).start()
    for j in range(units):
        if j == 2:
            for i in range(splits):
                got_copy(1, i).start()
        for which in range(3):
            w_copy(which, j).start()

    def split_rows(group, i):
        cols = block(split, i)
        both = got_v[group][:, :, cols].astype(F32)
        x_v[group][:, cols] = both[:, :RANKS].reshape(rows, split).astype(BF16)
        dy_v[group][:, cols] = both[:, RANKS:].reshape(rows, split).astype(BF16)

    @pl.loop(0, splits)
    def _(i):
        got_copy(0, i).wait()
        split_rows(0, i)

    wide = 2 * unit
    for group in range(2):
        here = block(rows, group)

        @pl.loop(0, hid // wide)
        def _(j):
            if group == 0:
                for part in range(2):
                    for which in range(3):
                        w_copy(which, 2 * j + part).wait()
            cols = block(wide, j)
            g = jnp.dot(x_v[group][...], wg_v[:, cols], preferred_element_type=F32)
            u = jnp.dot(x_v[group][...], wu_v[:, cols], preferred_element_type=F32)
            sig = jax.nn.sigmoid(g)
            silu = g * sig
            h_v[here, cols] = (silu * u).astype(BF16)
            slope = u * sig * (1.0 + g * (1.0 - sig))
            dh = lax.dot_general(
                dy_v[group][...], wd_v[cols, :], CONTRACT_LAST, preferred_element_type=F32
            )
            dg_v[here, cols] = (dh * slope).astype(BF16)
            du_v[here, cols] = (dh * silu).astype(BF16)

        for copy in row_copies(group) + hid_copies(group):
            copy.start()
        if group == 0:

            @pl.loop(0, splits)
            def _(i):
                got_copy(1, i).wait()
                split_rows(1, i)

    half = width // 2

    @pl.loop(0, half // out)
    def _(i):
        parts = []
        for side in range(2):
            at = block(out, side * (half // out) + i)
            part = lax.dot_general(
                dg_v[...], wg_v[at, :], CONTRACT_LAST, preferred_element_type=F32
            ) + lax.dot_general(du_v[...], wu_v[at, :], CONTRACT_LAST, preferred_element_type=F32)
            parts.append(part.reshape(2 * peers, RANKS, out))
        dx_v[:, :, block(out, i)] = jnp.concatenate(parts, axis=1).astype(BF16)
        for copy in dx_copies(i):
            copy.start()

    for copy in [c for group in range(2) for c in row_copies(group) + hid_copies(group)]:
        copy.wait()
    for copy in [c for i in range(half // out) for c in dx_copies(i)]:
        copy.wait()


def hidden_pass(got0, got1, wg, wu, wd):
    peers, _, width = got0.shape
    hid = wg.shape[1]
    rows = 2 * peers * RANKS
    splits, units = width // 512, hid // 256
    wide, narrow = (jax.ShapeDtypeStruct((rows, n), BF16) for n in (width, hid))
    dx = jax.ShapeDtypeStruct((peers, ROWS, width // 2), BF16)
    return pl.pallas_call(
        hidden_kernel,
        in_specs=[pl.BlockSpec(memory_space=pl.ANY)] * 5,
        out_specs=[pl.BlockSpec(memory_space=pl.ANY)] * 7,
        out_shape=[wide, wide, narrow, narrow, narrow, dx, dx],
        scratch_shapes=[
            pltpu.VMEM((peers, ROWS, width), BF16),
            pltpu.VMEM((peers, ROWS, width), BF16),
            pltpu.VMEM((width, hid), BF16),
            pltpu.VMEM((width, hid), BF16),
            pltpu.VMEM((hid, width), BF16),
            pltpu.VMEM((rows // 2, width), BF16),
            pltpu.VMEM((rows // 2, width), BF16),
            pltpu.VMEM((rows // 2, width), BF16),
            pltpu.VMEM((rows // 2, width), BF16),
            pltpu.VMEM((rows, hid), BF16),
            pltpu.VMEM((rows, hid), BF16),
            pltpu.VMEM((rows, hid), BF16),
            pltpu.VMEM((2 * peers, ROWS, width // 2), BF16),
            pltpu.SemaphoreType.DMA((2, splits)),
            pltpu.SemaphoreType.DMA((3, units)),
            pltpu.SemaphoreType.DMA((2, 2)),
            pltpu.SemaphoreType.DMA((3, 2)),
            pltpu.SemaphoreType.DMA((2, width // 1024)),
        ],
        compiler_params=params(60),
        cost_estimate=cost(2 * 5 * rows * width * hid, 36, rows * hid),
        name="hidden",
    )(got0, got1, wg, wu, wd)


def add_kernel(a_ref, b_ref, out_ref, sums, sem):
    parts = sem.shape[0]
    size = sums.shape[0] // parts
    copies = []
    for n in range(parts):
        at = block(size, n)
        sums[at] = (a_ref[at].astype(F32) + b_ref[at].astype(F32)).astype(BF16)
        copies.append(pltpu.make_async_copy(sums.at[at], out_ref.at[at], sem.at[n]))
        copies[-1].start()
    for copy in copies:
        copy.wait()


def add(a, b):
    return pl.pallas_call(
        add_kernel,
        in_specs=[pl.BlockSpec(memory_space=pltpu.VMEM)] * 2,
        out_specs=pl.BlockSpec(memory_space=pl.ANY),
        out_shape=jax.ShapeDtypeStruct(a.shape, BF16),
        scratch_shapes=[pltpu.VMEM(a.shape, BF16), pltpu.SemaphoreType.DMA((4,))],
        compiler_params=params(32),
        cost_estimate=cost(0, 6, 0),
        name="add",
    )(a, b)


def early_grads_kernel(x_ref, dy_ref, dg_ref, h_ref, gate_ref, down_ref):
    for left, right, out in ((x_ref, dg_ref, gate_ref), (dy_ref, h_ref, down_ref)):
        out[...] = lax.dot_general(
            left[...], right[...], CONTRACT_ROWS, preferred_element_type=F32
        )


def early_grads(x, dy, dg, h):
    rows, width = dy.shape
    hid = h.shape[1]
    cols = 512
    narrow = pl.BlockSpec((rows, cols), lambda i: (0, i))
    whole = pl.BlockSpec((rows, hid), lambda i: (0, 0))
    tall = pl.BlockSpec((cols, hid), lambda i: (i, 0))
    return pl.pallas_call(
        early_grads_kernel,
        grid=(width // cols,),
        in_specs=[narrow, narrow, whole, whole],
        out_specs=[tall, tall],
        out_shape=[jax.ShapeDtypeStruct((width, hid), F32)] * 2,
        compiler_params=params(60),
        cost_estimate=cost(2 * 2 * rows * width * hid, 28, 0),
        name="early_grads",
    )(x, dy, dg, h)


def weight_grads_kernel(
    x0_ref, x1_ref, dy_ref, gate0_ref, down0_ref, dg1, du0, du1, h1, gate_ref, up_ref, down_ref,
    dg1_v, du0_v, du1_v, h1_v, sem,
):
    whole = ((dg1, dg1_v), (du0, du0_v), (du1, du1_v), (h1, h1_v))
    copies = [pltpu.make_async_copy(src, dst, sem.at[n]) for n, (src, dst) in enumerate(whole)]
    first = pl.program_id(0) == 0

    @pl.when(first)
    def _():
        for copy in copies:
            copy.start()

    def arrived(*numbers):
        @pl.when(first)
        def _():
            for n in numbers:
                copies[n].wait()

    def term(left, right):
        return lax.dot_general(
            left[...], right[...], CONTRACT_ROWS, preferred_element_type=F32
        )

    arrived(0)
    gate_ref[...] = (gate0_ref[...] + term(x1_ref, dg1_v)).astype(BF16)
    arrived(1, 2)
    up_ref[...] = (term(x0_ref, du0_v) + term(x1_ref, du1_v)).astype(BF16)
    arrived(3)
    down_ref[...] = (down0_ref[...] + term(dy_ref, h1_v)).T.astype(BF16)


def weight_grads(x, du, dg1, dy1, h1, early):
    rows, width = dy1.shape
    hid = h1.shape[1]
    cols = 512
    narrow = pl.BlockSpec((rows, cols), lambda i: (0, i))
    tall = pl.BlockSpec((cols, hid), lambda i: (i, 0))
    flat = jax.ShapeDtypeStruct((width, hid), BF16)
    return pl.pallas_call(
        weight_grads_kernel,
        grid=(width // cols,),
        in_specs=[narrow] * 3 + [tall] * 2 + [pl.BlockSpec(memory_space=pl.ANY)] * 4,
        out_specs=[tall, tall, pl.BlockSpec((hid, cols), lambda i: (0, i))],
        out_shape=[flat, flat, jax.ShapeDtypeStruct((hid, width), BF16)],
        scratch_shapes=[pltpu.VMEM((rows, hid), BF16)] * 4 + [pltpu.SemaphoreType.DMA((4,))],
        compiler_params=params(60),
        cost_estimate=cost(2 * 4 * rows * width * hid, 48, 0),
        name="weight_grads",
    )(*x, dy1, *early, dg1, *du, h1)


def collect_kernel(chunk, experts, ids_ref, back_ref, *refs):
    tok = ids_ref.shape[1]
    half = back_ref.shape[2]
    lane = lax.broadcasted_iota(jnp.int32, (tok, experts * ROWS), 1)
    slots = [as_column(slot) for slot in route_slots(ids_ref, experts, chunk)]
    dx = (back_ref[:experts].astype(F32) + back_ref[experts:].astype(F32)).astype(BF16)
    dx = dx.reshape(experts * ROWS, half)
    for side in range(2):
        cols = slice(side * half, (side + 1) * half)
        pick = jnp.zeros((tok, experts * ROWS), jnp.bool_)
        for slot in slots:
            pick = pick | (lane == jnp.where(slot >= 0, slot + side * RANKS, -1))
        total = jnp.dot(pick.astype(BF16), dx, preferred_element_type=F32)
        if len(refs) > 1:
            total = refs[0][:, cols] + total
        refs[-1][:, cols] = total.astype(refs[-1].dtype)


def collect(chunk, experts, ids, back, before=None):
    tok = ids.shape[1]
    half = back.shape[2]
    more = () if before is None else (before,)
    return pl.pallas_call(
        lambda *refs: collect_kernel(chunk, experts, *refs),
        in_specs=[pl.BlockSpec(memory_space=pltpu.VMEM)] * (2 + len(more)),
        out_specs=pl.BlockSpec(memory_space=pltpu.VMEM),
        out_shape=jax.ShapeDtypeStruct((tok, 2 * half), BF16 if more else F32),
        compiler_params=params(24),
        cost_estimate=cost(2 * 2 * tok * experts * ROWS * half, 4, 0),
        name="collect",
    )(ids, back, *more)


def exchange(rows):
    return lax.all_to_all(rows, PEERS, split_axis=0, concat_axis=0, tiled=True)


def other_core(rows):
    return lax.ppermute(rows, "core", [(0, 1), (1, 0)])


def shards(tokens, grad_out, gates, expert_ids, w_gate, w_up, w_down):
    experts = lax.axis_size(EXPERT)
    wg, wu, wd = w_gate[0], w_up[0], w_down[0]
    ids, scales = expert_ids.T, gates.T
    sends = [pack(chunk, experts, ids, scales, tokens, grad_out) for chunk in range(2)]
    got0, send1 = lax.optimization_barrier((exchange(sends[0]), sends[1]))
    got = [got0, exchange(send1)]
    x, du, back = [], [], []
    for chunk in range(2):
        rows = got[chunk]
        if chunk:
            rows, early, dx = lax.optimization_barrier((rows, early, dx))
        now = hidden_pass(other_core(rows), rows, wg, wu, wd)
        x.append(now[0])
        du.append(now[4])
        theirs = now[5]
        if chunk:
            first, theirs = lax.optimization_barrier((back[0], theirs))
            part = collect(0, experts, ids, first)
        sent = other_core(theirs)
        if chunk:
            sent, part = lax.optimization_barrier((sent, part))
        else:
            early = early_grads(now[0], now[1], now[3], now[2])
            sent, early = lax.optimization_barrier((sent, early))
        dx = add(now[6], sent)
        back.append(exchange(dx))
    x[1], _ = lax.optimization_barrier((x[1], dx))
    grad_gate, grad_up, down = weight_grads(x, du, now[3], now[1], now[2], early)
    grad_tokens = collect(1, experts, ids, back[1], part)
    return (grad_tokens, grad_gate[None], grad_up[None], down[None])


def solution(mesh):
    fine = Mesh(mesh.devices.reshape(2, 2, 4, 4, 2), DEVICE)
    per_token = P(DEVICE, None)
    columns = P(EXPERT, None, ("yhi", "core"))
    rows = P(EXPERT, ("yhi", "core"), None)
    return jax.shard_map(
        shards,
        mesh=fine,
        in_specs=(per_token,) * 4 + (columns, columns, rows),
        out_specs=(per_token, columns, columns, rows),
        check_vma=False,
    )
```

```python
import jax
import jax.numpy as jnp
from jax import lax
from jax.experimental import pallas as pl
from jax.experimental.pallas import tpu as pltpu
from jax.sharding import Mesh, PartitionSpec as P

DEVICE = ("yhi", "core", "x", "z", "ylo")
EXPERT = ("x", "z", "ylo")
PEERS = ("yhi", "x", "z", "ylo")

BF16 = jnp.bfloat16
F32 = jnp.float32
RANKS = 8
ROWS = 2 * RANKS
MIB = 1024 * 1024

CONTRACT_LAST = (((1,), (1,)), ((), ()))
CONTRACT_ROWS = (((0,), (0,)), ((), ()))


def params(mib):
    return pltpu.CompilerParams(vmem_limit_bytes=mib * MIB)


def route_slots(ids_ref, experts, chunk):
    tok = ids_ref.shape[1]
    expert = lax.broadcasted_iota(jnp.int32, (experts, tok), 0)
    picks = [(ids_ref[k : k + 1, :] == expert).astype(F32) for k in range(2)]
    before = lax.broadcasted_iota(jnp.int32, (tok, tok), 0) < lax.broadcasted_iota(
        jnp.int32, (tok, tok), 1
    )
    ahead = jnp.dot(
        (picks[0] + picks[1]).astype(BF16), before.astype(BF16), preferred_element_type=F32
    )
    slots = []
    for k in range(2):
        rank = jnp.sum(ahead * picks[k], axis=0, keepdims=True).astype(jnp.int32) - chunk * RANKS
        inside = (rank >= 0) & (rank < RANKS)
        slots.append(jnp.where(inside, ids_ref[k : k + 1, :] * ROWS + rank, -1))
    return slots


def as_column(row):
    size = row.shape[1]
    same = lax.broadcasted_iota(jnp.int32, (size, size), 0) == lax.broadcasted_iota(
        jnp.int32, (size, size), 1
    )
    return jnp.sum(jnp.where(same, row, jnp.zeros_like(row)), axis=1, keepdims=True)


def pack_kernel(chunk, experts, ids_ref, gates_ref, tok_ref, grad_ref, out, pick, rows, packed, sem):
    tok, width = tok_ref.shape
    cols = 512
    slots = route_slots(ids_ref, experts, chunk)
    at = lax.broadcasted_iota(jnp.int32, (experts * ROWS, tok), 0)
    pick[:, :tok] = ((at == slots[0]) | (at == slots[1])).astype(BF16)
    rows[:tok] = tok_ref[...]
    for k in range(2):
        here = slice((1 + k) * tok, (2 + k) * tok)
        there = jnp.where(slots[k] >= 0, slots[k] + RANKS, -1)
        pick[:, here] = (at == there).astype(BF16)
        gate = as_column(gates_ref[k : k + 1, :])
        rows[here] = (gate * grad_ref[...].astype(F32)).astype(BF16)

    copies = []
    for i in range(width // cols):
        part = block(cols, i)
        packed[:, :, part] = (
            jnp.dot(pick[...], rows[:, part], preferred_element_type=F32)
            .astype(BF16)
            .reshape(experts, ROWS, cols)
        )
        for yhi in range(2):
            copies.append(
                pltpu.make_async_copy(
                    packed.at[:, :, part], out.at[block(experts, yhi), :, part], sem.at[yhi, i]
                )
            )
            copies[-1].start()
    for copy in copies:
        copy.wait()


def pack(chunk, experts, ids, gates, tokens, grad_out):
    tok, width = tokens.shape
    return pl.pallas_call(
        lambda *refs: pack_kernel(chunk, experts, *refs),
        in_specs=[pl.BlockSpec(memory_space=pltpu.VMEM)] * 4,
        out_specs=pl.BlockSpec(memory_space=pl.ANY),
        out_shape=jax.ShapeDtypeStruct((2 * experts, ROWS, width), BF16),
        scratch_shapes=[
            pltpu.VMEM((experts * ROWS, 3 * tok), BF16),
            pltpu.VMEM((3 * tok, width), BF16),
            pltpu.VMEM((experts, ROWS, width), BF16),
            pltpu.SemaphoreType.DMA((2, width // 512)),
        ],
        compiler_params=params(60),
        cost_estimate=cost(2 * 3 * tok * experts * ROWS * width, 12, 0),
        name="pack",
    )(ids, gates, tokens, grad_out)


def block(size, index):
    return pl.ds(index * size if isinstance(index, int) else pl.multiple_of(index * size, size), size)


def cost(flops, mib, transcendentals=0):
    return pl.CostEstimate(
        flops=flops // 8, bytes_accessed=mib * MIB // 8, transcendentals=transcendentals // 8
    )


def hidden_kernel(
    got0, got1, wg, wu, wd, x, dy, h, dg, du, dx0, dx1,
    got_v0, got_v1, wg_v, wu_v, wd_v, x_v0, x_v1, dy_v0, dy_v1, h_v, dg_v, du_v, dx_v,
    got_sem, w_sem, row_sem, hid_sem, dx_sem,
):
    got, got_v = (got0, got1), (got_v0, got_v1)
    x_v, dy_v = (x_v0, x_v1), (dy_v0, dy_v1)
    peers, _, width = got0.shape
    hid = wg.shape[1]
    rows = peers * RANKS
    split, out, unit = 512, 512, 256
    splits, units = width // split, hid // unit

    def got_copy(group, i):
        at = (slice(None), slice(None), block(split, i))
        return pltpu.make_async_copy(
            got[group].at[at], got_v[group].at[at], got_sem.at[group, i]
        )

    def w_copy(which, j):
        src, dst = ((wg, wg_v), (wu, wu_v), (wd, wd_v))[which]
        at = (block(unit, j), slice(None)) if which == 2 else (slice(None), block(unit, j))
        return pltpu.make_async_copy(src.at[at], dst.at[at], w_sem.at[which, j])

    def row_copies(group):
        at = (block(rows, group), slice(None))
        return [
            pltpu.make_async_copy(src[group], dst.at[at], row_sem.at[n, group])
            for n, (src, dst) in enumerate(((x_v, x), (dy_v, dy)))
        ]

    def hid_copies(group):
        at = (block(rows, group), slice(None))
        return [
            pltpu.make_async_copy(src.at[at], dst.at[at], hid_sem.at[n, group])
            for n, (src, dst) in enumerate(((h_v, h), (dg_v, dg), (du_v, du)))
        ]

    def dx_copies(i):
        cols = block(out, i)
        return [
            pltpu.make_async_copy(
                dx_v.at[block(peers, n), :, cols], dx.at[:, :, cols], dx_sem.at[n, i]
            )
            for n, dx in enumerate((dx0, dx1))
        ]

    for i in range(splits):
        got_copy(0, i).start()
    for j in range(units):
        if j == 2:
            for i in range(splits):
                got_copy(1, i).start()
        for which in range(3):
            w_copy(which, j).start()

    def split_rows(group, i):
        cols = block(split, i)
        both = got_v[group][:, :, cols].astype(F32)
        x_v[group][:, cols] = both[:, :RANKS].reshape(rows, split).astype(BF16)
        dy_v[group][:, cols] = both[:, RANKS:].reshape(rows, split).astype(BF16)

    @pl.loop(0, splits)
    def _(i):
        got_copy(0, i).wait()
        split_rows(0, i)

    wide = 2 * unit
    for group in range(2):
        here = block(rows, group)

        @pl.loop(0, hid // wide)
        def _(j):
            if group == 0:
                for part in range(2):
                    for which in range(3):
                        w_copy(which, 2 * j + part).wait()
            cols = block(wide, j)
            g = jnp.dot(x_v[group][...], wg_v[:, cols], preferred_element_type=F32)
            u = jnp.dot(x_v[group][...], wu_v[:, cols], preferred_element_type=F32)
            sig = jax.nn.sigmoid(g)
            silu = g * sig
            h_v[here, cols] = (silu * u).astype(BF16)
            slope = u * sig * (1.0 + g * (1.0 - sig))
            dh = lax.dot_general(
                dy_v[group][...], wd_v[cols, :], CONTRACT_LAST, preferred_element_type=F32
            )
            dg_v[here, cols] = (dh * slope).astype(BF16)
            du_v[here, cols] = (dh * silu).astype(BF16)

        for copy in row_copies(group) + hid_copies(group):
            copy.start()
        if group == 0:

            @pl.loop(0, splits)
            def _(i):
                got_copy(1, i).wait()
                split_rows(1, i)

    half = width // 2

    @pl.loop(0, half // out)
    def _(i):
        parts = []
        for side in range(2):
            at = block(out, side * (half // out) + i)
            part = lax.dot_general(
                dg_v[...], wg_v[at, :], CONTRACT_LAST, preferred_element_type=F32
            ) + lax.dot_general(du_v[...], wu_v[at, :], CONTRACT_LAST, preferred_element_type=F32)
            parts.append(part.reshape(2 * peers, RANKS, out))
        dx_v[:, :, block(out, i)] = jnp.concatenate(parts, axis=1).astype(BF16)
        for copy in dx_copies(i):
            copy.start()

    for copy in [c for group in range(2) for c in row_copies(group) + hid_copies(group)]:
        copy.wait()
    for copy in [c for i in range(half // out) for c in dx_copies(i)]:
        copy.wait()


def hidden_pass(got0, got1, wg, wu, wd):
    peers, _, width = got0.shape
    hid = wg.shape[1]
    rows = 2 * peers * RANKS
    splits, units = width // 512, hid // 256
    wide, narrow = (jax.ShapeDtypeStruct((rows, n), BF16) for n in (width, hid))
    dx = jax.ShapeDtypeStruct((peers, ROWS, width // 2), BF16)
    return pl.pallas_call(
        hidden_kernel,
        in_specs=[pl.BlockSpec(memory_space=pl.ANY)] * 5,
        out_specs=[pl.BlockSpec(memory_space=pl.ANY)] * 7,
        out_shape=[wide, wide, narrow, narrow, narrow, dx, dx],
        scratch_shapes=[
            pltpu.VMEM((peers, ROWS, width), BF16),
            pltpu.VMEM((peers, ROWS, width), BF16),
            pltpu.VMEM((width, hid), BF16),
            pltpu.VMEM((width, hid), BF16),
            pltpu.VMEM((hid, width), BF16),
            pltpu.VMEM((rows // 2, width), BF16),
            pltpu.VMEM((rows // 2, width), BF16),
            pltpu.VMEM((rows // 2, width), BF16),
            pltpu.VMEM((rows // 2, width), BF16),
            pltpu.VMEM((rows, hid), BF16),
            pltpu.VMEM((rows, hid), BF16),
            pltpu.VMEM((rows, hid), BF16),
            pltpu.VMEM((2 * peers, ROWS, width // 2), BF16),
            pltpu.SemaphoreType.DMA((2, splits)),
            pltpu.SemaphoreType.DMA((3, units)),
            pltpu.SemaphoreType.DMA((2, 2)),
            pltpu.SemaphoreType.DMA((3, 2)),
            pltpu.SemaphoreType.DMA((2, width // 1024)),
        ],
        compiler_params=params(60),
        cost_estimate=cost(2 * 5 * rows * width * hid, 36, rows * hid),
        name="hidden",
    )(got0, got1, wg, wu, wd)


def add_kernel(a_ref, b_ref, out_ref, sums, sem):
    parts = sem.shape[0]
    size = sums.shape[0] // parts
    copies = []
    for n in range(parts):
        at = block(size, n)
        sums[at] = (a_ref[at].astype(F32) + b_ref[at].astype(F32)).astype(BF16)
        copies.append(pltpu.make_async_copy(sums.at[at], out_ref.at[at], sem.at[n]))
        copies[-1].start()
    for copy in copies:
        copy.wait()


def add(a, b):
    return pl.pallas_call(
        add_kernel,
        in_specs=[pl.BlockSpec(memory_space=pltpu.VMEM)] * 2,
        out_specs=pl.BlockSpec(memory_space=pl.ANY),
        out_shape=jax.ShapeDtypeStruct(a.shape, BF16),
        scratch_shapes=[pltpu.VMEM(a.shape, BF16), pltpu.SemaphoreType.DMA((4,))],
        compiler_params=params(32),
        cost_estimate=cost(0, 6, 0),
        name="add",
    )(a, b)


def early_grads_kernel(x_ref, dy_ref, dg_ref, h_ref, gate_ref, down_ref):
    for left, right, out in ((x_ref, dg_ref, gate_ref), (dy_ref, h_ref, down_ref)):
        out[...] = lax.dot_general(
            left[...], right[...], CONTRACT_ROWS, preferred_element_type=F32
        )


def early_grads(x, dy, dg, h):
    rows, width = dy.shape
    hid = h.shape[1]
    cols = 512
    narrow = pl.BlockSpec((rows, cols), lambda i: (0, i))
    whole = pl.BlockSpec((rows, hid), lambda i: (0, 0))
    tall = pl.BlockSpec((cols, hid), lambda i: (i, 0))
    return pl.pallas_call(
        early_grads_kernel,
        grid=(width // cols,),
        in_specs=[narrow, narrow, whole, whole],
        out_specs=[tall, tall],
        out_shape=[jax.ShapeDtypeStruct((width, hid), F32)] * 2,
        compiler_params=params(60),
        cost_estimate=cost(2 * 2 * rows * width * hid, 28, 0),
        name="early_grads",
    )(x, dy, dg, h)


def weight_grads_kernel(
    x0_ref, x1_ref, dy_ref, gate0_ref, down0_ref, dg1, du0, du1, h1, gate_ref, up_ref, down_ref,
    dg1_v, du0_v, du1_v, h1_v, sem,
):
    whole = ((dg1, dg1_v), (du0, du0_v), (du1, du1_v), (h1, h1_v))
    copies = [pltpu.make_async_copy(src, dst, sem.at[n]) for n, (src, dst) in enumerate(whole)]
    first = pl.program_id(0) == 0

    @pl.when(first)
    def _():
        for copy in copies:
            copy.start()

    def arrived(*numbers):
        @pl.when(first)
        def _():
            for n in numbers:
                copies[n].wait()

    def term(left, right):
        return lax.dot_general(
            left[...], right[...], CONTRACT_ROWS, preferred_element_type=F32
        )

    arrived(0)
    gate_ref[...] = (gate0_ref[...] + term(x1_ref, dg1_v)).astype(BF16)
    arrived(1, 2)
    up_ref[...] = (term(x0_ref, du0_v) + term(x1_ref, du1_v)).astype(BF16)
    arrived(3)
    down_ref[...] = (down0_ref[...] + term(dy_ref, h1_v)).T.astype(BF16)


def weight_grads(x, du, dg1, dy1, h1, early):
    rows, width = dy1.shape
    hid = h1.shape[1]
    cols = 256
    narrow = pl.BlockSpec((rows, cols), lambda i: (0, i))
    tall = pl.BlockSpec((cols, hid), lambda i: (i, 0))
    flat = jax.ShapeDtypeStruct((width, hid), BF16)
    return pl.pallas_call(
        weight_grads_kernel,
        grid=(width // cols,),
        in_specs=[narrow] * 3 + [tall] * 2 + [pl.BlockSpec(memory_space=pl.ANY)] * 4,
        out_specs=[tall, tall, pl.BlockSpec((hid, cols), lambda i: (0, i))],
        out_shape=[flat, flat, jax.ShapeDtypeStruct((hid, width), BF16)],
        scratch_shapes=[pltpu.VMEM((rows, hid), BF16)] * 4 + [pltpu.SemaphoreType.DMA((4,))],
        compiler_params=params(60),
        cost_estimate=cost(2 * 4 * rows * width * hid, 48, 0),
        name="weight_grads",
    )(*x, dy1, *early, dg1, *du, h1)


def collect_kernel(chunk, experts, ids_ref, back_ref, *refs):
    tok = ids_ref.shape[1]
    half = back_ref.shape[2]
    lane = lax.broadcasted_iota(jnp.int32, (tok, experts * ROWS), 1)
    slots = [as_column(slot) for slot in route_slots(ids_ref, experts, chunk)]
    dx = (back_ref[:experts].astype(F32) + back_ref[experts:].astype(F32)).astype(BF16)
    dx = dx.reshape(experts * ROWS, half)
    for side in range(2):
        cols = slice(side * half, (side + 1) * half)
        pick = jnp.zeros((tok, experts * ROWS), jnp.bool_)
        for slot in slots:
            pick = pick | (lane == jnp.where(slot >= 0, slot + side * RANKS, -1))
        total = jnp.dot(pick.astype(BF16), dx, preferred_element_type=F32)
        if len(refs) > 1:
            total = refs[0][:, cols] + total
        refs[-1][:, cols] = total.astype(refs[-1].dtype)


def collect(chunk, experts, ids, back, before=None):
    tok = ids.shape[1]
    half = back.shape[2]
    more = () if before is None else (before,)
    return pl.pallas_call(
        lambda *refs: collect_kernel(chunk, experts, *refs),
        in_specs=[pl.BlockSpec(memory_space=pltpu.VMEM)] * (2 + len(more)),
        out_specs=pl.BlockSpec(memory_space=pltpu.VMEM),
        out_shape=jax.ShapeDtypeStruct((tok, 2 * half), BF16 if more else F32),
        compiler_params=params(24),
        cost_estimate=cost(2 * 2 * tok * experts * ROWS * half, 4, 0),
        name="collect",
    )(ids, back, *more)


def exchange(rows):
    return lax.all_to_all(rows, PEERS, split_axis=0, concat_axis=0, tiled=True)


def other_core(rows):
    return lax.ppermute(rows, "core", [(0, 1), (1, 0)])


def shards(tokens, grad_out, gates, expert_ids, w_gate, w_up, w_down):
    experts = lax.axis_size(EXPERT)
    wg, wu, wd = w_gate[0], w_up[0], w_down[0]
    ids, scales = expert_ids.T, gates.T
    sends = [pack(chunk, experts, ids, scales, tokens, grad_out) for chunk in range(2)]
    got0, send1 = lax.optimization_barrier((exchange(sends[0]), sends[1]))
    got = [got0, exchange(send1)]
    x, du, back = [], [], []
    for chunk in range(2):
        rows = got[chunk]
        if chunk:
            rows, early, dx = lax.optimization_barrier((rows, early, dx))
        now = hidden_pass(other_core(rows), rows, wg, wu, wd)
        x.append(now[0])
        du.append(now[4])
        theirs = now[5]
        if chunk:
            first, theirs = lax.optimization_barrier((back[0], theirs))
            part = collect(0, experts, ids, first)
        sent = other_core(theirs)
        if chunk:
            sent, part = lax.optimization_barrier((sent, part))
        else:
            early = early_grads(now[0], now[1], now[3], now[2])
            sent, early = lax.optimization_barrier((sent, early))
        dx = add(now[6], sent)
        back.append(exchange(dx))
    x[1], _ = lax.optimization_barrier((x[1], dx))
    grad_gate, grad_up, down = weight_grads(x, du, now[3], now[1], now[2], early)
    grad_tokens = collect(1, experts, ids, back[1], part)
    return (grad_tokens, grad_gate[None], grad_up[None], down[None])


def solution(mesh):
    fine = Mesh(mesh.devices.reshape(2, 2, 4, 4, 2), DEVICE)
    per_token = P(DEVICE, None)
    columns = P(EXPERT, None, ("yhi", "core"))
    rows = P(EXPERT, ("yhi", "core"), None)
    return jax.shard_map(
        shards,
        mesh=fine,
        in_specs=(per_token,) * 4 + (columns, columns, rows),
        out_specs=(per_token, columns, columns, rows),
        check_vma=False,
    )
```
